256 devices in a mesh: gx: 4 (over x), gy: 8 (over z_hi, y), gz: 8 (over z_lo, core).
Axes of the slice: x: 4, y: 4, z: 8 (z_hi: 2, z_lo: 4; z = z_hi * 4 + z_lo), core: 2. Of those that a mesh axis runs over, the one named last changes fastest.
Arguments:
- features: bfloat16 [32768, 1536], P(('gx', 'gy', 'gz')), may hold values from -6 to 6
- species: int32 [32768], P(('gx', 'gy', 'gz')), may hold values from 0 to 88
- octant_lists: int32 [2, 2, 2, 2048], P(None, None, None, ('gx', 'gy', 'gz')), may hold values from 0 to 127
- neighbour_index: int32 [32, 32768], P(None, ('gx', 'gy', 'gz')), may hold values from 0 to 319
- neighbour_count: int32 [32768], P(('gx', 'gy', 'gz')), may hold values from 16 to 32
- edge_vectors: float32 [3, 32, 32768], P(None, None, ('gx', 'gy', 'gz')), may hold values from -2.3 to 2.3
- radial_in: bfloat16 [3, 8, 64], replicated, may hold values from -3 to 3
- species_emb: bfloat16 [3, 89, 64], replicated, may hold values from -6 to 6
- radial_mid: bfloat16 [3, 64, 64], replicated, may hold values from -0.5 to 0.5
- radial_out: bfloat16 [3, 64, 384], replicated, may hold values from -0.75 to 0.75
- mix_weight: bfloat16 [3, 4, 96, 96], replicated, may hold values from -0.625 to 0.625
- gate_weight: bfloat16 [3, 96, 96], replicated, may hold values from -0.625 to 0.625
- probe_in: bfloat16 [8, 64], replicated, may hold values from -3 to 3
- probe_mid: bfloat16 [64, 64], replicated, may hold values from -0.5 to 0.5
- probe_proj: bfloat16 [4, 96, 64], replicated, may hold values from -0.01953125 to 0.01953125
- probe_vectors: float32 [3, 32, 32768], P(None, None, ('gx', 'gy', 'gz')), may hold values from -2.3 to 2.3
- probe_index: int32 [32, 32768], P(None, ('gx', 'gy', 'gz')), may hold values from 0 to 319
- probe_count: int32 [32768], P(('gx', 'gy', 'gz')), may hold values from 16 to 32
- slab_index: int32 [32], replicated, may hold values from 0 to 7
Outputs:
- atom_features: bfloat16 [32768, 1536], P(('gx', 'gy', 'gz'))
- density: float32 [32768], P(('gx', 'gy', 'gz'))
The draws below stay inside these ranges and needn't reach their ends.
Inputs may be any that keep to these rules, and one draw needn't show every extreme that they name: `neighbour_index`: rows 0 to 127 of a table are the brick's own atoms, then 24 * 8 ghost rows in the order of the steps. Slots k >= neighbour_count of an atom are padding. `probe_index`: slots k >= probe_count of a probe are padding; rows refer to the table of the slab brick of the probe's column.
All inputs are finite; a program needn't handle non-finite values.
Results may differ from the reference program's by a relative error of at most 0.019.
Values may be sent and summed in bfloat16 or wider, within the bound.
No kernel may reach another device: no remote copies, remote signals or barrier semaphores. Data moves between devices by JAX's collectives and lax.ppermute only.
A program may use at most 128 MiB of HBM per device.

```python
import math
import jax
import jax.numpy as jnp
import numpy as np
from jax import lax

C = 96
COMPS = 16
RH = 64
NB = 8
SPECIES = 89
K = 32
KP = 32
LAYERS = 3
A_DEV = 128
P_DEV = 128
GO = 8
TABLE = 320
ATOMS = 32768
PROBES = 32768
LISTS = 2048
BRICKS_Z = 8
COLUMNS = 32
N_GX = 4
N_GY = 8
N_GZ = 8


def place_ends(values, stream_key, least, high):
    longest = values.shape.index(max(values.shape))
    spots = []
    for shift in (0, 1):
        where = [jax.random.randint(jax.random.fold_in(stream_key, axis), (), 0, length) for axis, length in enumerate(values.shape)]
        where[longest] = (where[longest] + shift) % values.shape[longest]
        spots.append(tuple(where))
    return values.at[spots[0]].set(least).at[spots[1]].set(high)


def block_levels(key, dims, cuts, smallest, largest):
    gain, own = 1.0, jax.random.fold_in(key, 6)
    for position, shards_of in cuts:
        heights = jnp.exp(jax.random.uniform(jax.random.fold_in(own, position), (shards_of,), jnp.float32, smallest / len(cuts), largest / len(cuts)))
        gain = gain * jnp.repeat(heights, dims[position] // shards_of).reshape([-1 if axis == position else 1 for axis in range(len(dims))])
    return gain


def bell_draw(rng, dims, spread, bound, cuts=(), kind=jnp.bfloat16):
    values = jax.random.normal(rng, dims, jnp.float32) * spread
    if len(cuts) > 0:
        values = block_levels(rng, dims, cuts, -0.22, 0.18) * values
    return jnp.clip(values, min=-bound, max=bound).astype(kind)


def setup_inputs(seed: int = 0) -> dict:
    key_of = jax.random.split(jax.random.key(seed), 20)
    return {
        "features": bell_draw(key_of[0], (ATOMS, COMPS * C), 1.0, 6.0, ((0, 256),)),
        "species": place_ends(jax.random.randint(key_of[1], (ATOMS,), 0, SPECIES), jax.random.fold_in(key_of[1], 1), 0, SPECIES - 1).astype(jnp.int32),
        "octant_lists": place_ends(jax.random.randint(key_of[2], (2, 2, 2, LISTS), 0, A_DEV), jax.random.fold_in(key_of[2], 1), 0, A_DEV - 1).astype(jnp.int32),
        "neighbour_index": place_ends(jax.random.randint(key_of[3], (K, ATOMS), 0, TABLE), jax.random.fold_in(key_of[3], 1), 0, TABLE - 1).astype(jnp.int32),
        "neighbour_count": place_ends(jax.random.randint(key_of[4], (ATOMS,), K // 2, K + 1), jax.random.fold_in(key_of[4], 1), K // 2, K).astype(jnp.int32),
        "edge_vectors": jnp.clip(jax.random.uniform(key_of[5], (3, K, ATOMS), jnp.float32, -2.3, 2.3) * block_levels(key_of[5], (3, K, ATOMS), ((2, 256),), -0.4, 0.0), -2.3, 2.3),
        "radial_in": jnp.clip(jax.random.uniform(key_of[6], (LAYERS, NB, RH), jnp.float32, -3.0, 3.0), -3.0, 3.0).astype(jnp.bfloat16),
        "species_emb": bell_draw(key_of[7], (LAYERS, SPECIES, RH), 1.0, 6.0),
        "radial_mid": jnp.clip(jax.random.uniform(key_of[8], (LAYERS, RH, RH), jnp.float32, -0.5, 0.5), -0.5, 0.5).astype(jnp.bfloat16),
        "radial_out": bell_draw(key_of[9], (LAYERS, RH, 4 * C), RH ** -0.5, 0.75),
        "mix_weight": bell_draw(key_of[10], (LAYERS, 4, C, C), C ** -0.5, 0.625),
        "gate_weight": bell_draw(key_of[11], (LAYERS, C, C), C ** -0.5, 0.625),
        "probe_in": jnp.clip(jax.random.uniform(key_of[12], (NB, RH), jnp.float32, -3.0, 3.0), -3.0, 3.0).astype(jnp.bfloat16),
        "probe_mid": jnp.clip(jax.random.uniform(key_of[13], (RH, RH), jnp.float32, -0.5, 0.5), -0.5, 0.5).astype(jnp.bfloat16),
        "probe_proj": bell_draw(key_of[14], (4, C, RH), (16 * C * RH) ** -0.5, 0.01953125),
        "probe_vectors": jnp.clip(jax.random.uniform(key_of[15], (3, KP, PROBES), jnp.float32, -2.3, 2.3) * block_levels(key_of[15], (3, KP, PROBES), ((2, 256),), -0.4, 0.0), -2.3, 2.3),
        "probe_index": place_ends(jax.random.randint(key_of[16], (KP, PROBES), 0, TABLE), jax.random.fold_in(key_of[16], 1), 0, TABLE - 1).astype(jnp.int32),
        "probe_count": place_ends(jax.random.randint(key_of[17], (PROBES,), KP // 2, KP + 1), jax.random.fold_in(key_of[17], 1), KP // 2, KP).astype(jnp.int32),
        "slab_index": place_ends(jax.random.randint(key_of[18], (COLUMNS,), 0, BRICKS_Z), jax.random.fold_in(key_of[18], 1), 0, BRICKS_Z - 1).astype(jnp.int32),
    }


cutoff = 4.0
degree_of = np.repeat(np.arange(4), np.array([1, 3, 5, 7]))
degree_starts = (0, 1, 4, 9)
degree_widths = (1, 3, 5, 7)

def harmonics(vectors):
    coord_x = vectors[0] * 0.5
    coord_y = vectors[1] * 0.5
    coord_z = vectors[2] * 0.5
    square = coord_x * coord_x + coord_y * coord_y + coord_z * coord_z
    zz_term = 5.0 * coord_z * coord_z - square
    comps_list = [jnp.ones_like(coord_x), math.sqrt(3.0) * coord_x, math.sqrt(3.0) * coord_y, math.sqrt(3.0) * coord_z, math.sqrt(15.0) * coord_x * coord_y, math.sqrt(15.0) * coord_y * coord_z, math.sqrt(5.0) / 2.0 * (3.0 * coord_z * coord_z - square), math.sqrt(15.0) * coord_x * coord_z, math.sqrt(15.0) / 2.0 * (coord_x * coord_x - coord_y * coord_y), math.sqrt(35.0 / 8.0) * coord_y * (3.0 * coord_x * coord_x - coord_y * coord_y), math.sqrt(105.0) * coord_x * coord_y * coord_z, math.sqrt(21.0 / 8.0) * coord_y * zz_term, math.sqrt(7.0) / 2.0 * coord_z * (5.0 * coord_z * coord_z - 3.0 * square), math.sqrt(21.0 / 8.0) * coord_x * zz_term, math.sqrt(105.0) / 2.0 * coord_z * (coord_x * coord_x - coord_y * coord_y), math.sqrt(35.0 / 8.0) * coord_x * (coord_x * coord_x - 3.0 * coord_y * coord_y)]
    return jnp.stack(comps_list, axis=-1)

def geometry(vectors):
    square = lax.optimization_barrier(jnp.sum(vectors * vectors, axis=0))
    envelope = (1.0 - square / (cutoff * cutoff)) ** 2
    radius = jnp.sqrt(square)
    centers = jnp.arange(NB, dtype=jnp.float32) * (cutoff / (NB - 1))
    sharpness = ((NB - 1) / cutoff) ** 2
    radial_basis = jnp.exp(-sharpness * (radius[..., None] - centers) ** 2).astype(jnp.bfloat16)
    return (radial_basis, envelope, harmonics(vectors))

def degree_messages(gathered, radial4, harmonic):
    scalars = gathered[:, :, 0, :]
    pieces = []
    for degree in range(4):
        start = degree_starts[degree]
        width = degree_widths[degree]
        weight_here = radial4[:, :, degree, :]
        segment = gathered[:, :, start:start + width, :]
        piece = jnp.einsum('krmc,krc->rmc', segment, weight_here)
        if degree > 0:
            piece = piece + jnp.einsum('krc,krm->rmc', scalars * weight_here, harmonic[:, :, start:start + width])
        pieces.append(piece)
    return jnp.concatenate(pieces, axis=1)

def layer_rows(table_rows, own_rows, species, index_rows, count_rows, vector_rows, weights):
    radial_in, species_emb, radial_mid, radial_out, mix_weight, gate_weight = weights
    slot_count, row_count = index_rows.shape
    radial_basis, envelope, harmonic = geometry(vector_rows)
    onehot = (species[:, None] == jnp.arange(SPECIES, dtype=jnp.int32)[None, :]).astype(jnp.bfloat16)
    embedded = jnp.dot(onehot, species_emb, preferred_element_type=jnp.float32)
    hidden_one = jnp.einsum('krb,bh->krh', radial_basis.astype(jnp.float32), radial_in.astype(jnp.float32))
    hidden_one = jax.nn.silu(hidden_one + embedded[None]).astype(jnp.bfloat16)
    hidden_two = jnp.einsum('krh,hg->krg', hidden_one.astype(jnp.float32), radial_mid.astype(jnp.float32))
    hidden_two = jax.nn.silu(hidden_two).astype(jnp.bfloat16)
    radial = jnp.einsum('krg,go->kro', hidden_two.astype(jnp.float32), radial_out.astype(jnp.float32))
    valid_mask = (jnp.arange(slot_count, dtype=jnp.int32)[:, None] < count_rows[None, :]).astype(jnp.float32)
    radial = radial * (envelope * valid_mask)[..., None]
    radial4 = radial.reshape(slot_count, row_count, 4, C)
    gathered = jnp.take(table_rows, index_rows, axis=0).astype(jnp.float32).reshape(slot_count, row_count, COMPS, C)
    message = (degree_messages(gathered, radial4, harmonic) * K ** (-0.5)).astype(jnp.bfloat16)
    mixed_rows = jnp.einsum('rmc,mcd->rmd', message.astype(jnp.float32), mix_weight[degree_of].astype(jnp.float32))
    gate_values = jax.nn.sigmoid(jnp.dot(message[:, 0, :], gate_weight, preferred_element_type=jnp.float32))
    previous = own_rows.astype(jnp.float32).reshape(row_count, COMPS, C)
    scalar_new = previous[:, :1, :] + jax.nn.silu(mixed_rows[:, :1, :])
    higher_new = previous[:, 1:, :] + gate_values[:, None, :] * mixed_rows[:, 1:, :]
    updated = jnp.concatenate([scalar_new, higher_new], axis=1)
    return updated.reshape(row_count, COMPS * C).astype(jnp.bfloat16)

def ghost_rows(send_rows):
    devices = N_GX * N_GY * N_GZ
    low_x = jnp.roll(send_rows, 1, axis=0)[:, :, :, 1]
    high_x = jnp.roll(send_rows, -1, axis=0)[:, :, :, 0]
    low_y = jnp.roll(send_rows, 1, axis=1)[:, :, :, :, 1]
    high_y = jnp.roll(send_rows, -1, axis=1)[:, :, :, :, 0]
    low_z = jnp.roll(send_rows, 1, axis=2)[:, :, :, :, :, 1]
    high_z = jnp.roll(send_rows, -1, axis=2)[:, :, :, :, :, 0]
    face_parts = [face_part.reshape(devices, 4 * GO, COMPS * C) for face_part in (low_x, high_x, low_y, high_y, low_z, high_z)]
    return jnp.concatenate(face_parts, axis=1)

def probe_rows(key_rows, vector_rows, index_rows, count_rows, probe_in, probe_mid):
    slot_count = index_rows.shape[0]
    radial_basis, envelope, harmonic = geometry(vector_rows)
    probe_one = jnp.einsum('kpb,bh->kph', radial_basis.astype(jnp.float32), probe_in.astype(jnp.float32))
    probe_one = jax.nn.silu(probe_one).astype(jnp.bfloat16)
    probe_two = jnp.einsum('kph,hg->kpg', probe_one.astype(jnp.float32), probe_mid.astype(jnp.float32))
    probe_two = jax.nn.silu(probe_two).astype(jnp.bfloat16)
    gathered = jnp.take(key_rows, index_rows, axis=0).astype(jnp.float32)
    inner_sum = jnp.einsum('kpmh,kph->kpm', gathered, probe_two.astype(jnp.float32))
    valid_mask = (jnp.arange(slot_count, dtype=jnp.int32)[:, None] < count_rows[None, :]).astype(jnp.float32)
    per_edge = lax.optimization_barrier(jnp.sum(inner_sum * harmonic, axis=-1)) * envelope * valid_mask
    return lax.optimization_barrier(jnp.sum(per_edge, axis=0)) * KP ** (-0.5)

def reference(features, species, octant_lists, neighbour_index, neighbour_count, edge_vectors, radial_in, species_emb, radial_mid, radial_out, mix_weight, gate_weight, probe_in, probe_mid, probe_proj, probe_vectors, probe_index, probe_count, slab_index):
    devices = N_GX * N_GY * N_GZ
    width_all = COMPS * C
    own_rows = features.reshape(devices, A_DEV, width_all)
    species_dev = species.reshape(devices, A_DEV)
    index_dev = jnp.transpose(neighbour_index.reshape(K, devices, A_DEV), (1, 0, 2))
    count_dev = neighbour_count.reshape(devices, A_DEV)
    vector_dev = jnp.transpose(edge_vectors.reshape(3, K, devices, A_DEV), (2, 0, 1, 3))
    list_rows = jnp.transpose(octant_lists.reshape(2, 2, 2, devices, GO), (3, 0, 1, 2, 4)).reshape(devices, 8 * GO)

    def refresh(current):
        picked = jax.vmap(lambda rows_here, picks_here: jnp.take(rows_here, picks_here, axis=0))(current, list_rows)
        return ghost_rows(picked.reshape(N_GX, N_GY, N_GZ, 2, 2, 2, GO, width_all))
    ghosts = refresh(own_rows)
    for layer_step in range(LAYERS):
        weights = (radial_in[layer_step], species_emb[layer_step], radial_mid[layer_step], radial_out[layer_step], mix_weight[layer_step], gate_weight[layer_step])

        def one_device(items):
            own_part, ghost_part, species_part, index_part, count_part, vector_part = items
            table_rows = jnp.concatenate([own_part, ghost_part], axis=0)
            return layer_rows(table_rows, own_part, species_part, index_part, count_part, vector_part, weights)
        own_rows = lax.map(one_device, (own_rows, ghosts, species_dev, index_dev, count_dev, vector_dev))
        ghosts = refresh(own_rows)
    atom_features = own_rows.reshape(ATOMS, width_all)
    proj_full = probe_proj[degree_of].astype(jnp.float32)

    def project(items):
        own_part, ghost_part = items
        table_rows = jnp.concatenate([own_part, ghost_part], axis=0).astype(jnp.float32).reshape(TABLE, COMPS, C)
        return jnp.einsum('rmc,mch->rmh', table_rows, proj_full).astype(jnp.bfloat16)
    projections = lax.map(project, (own_rows, ghosts))
    root_grid = projections.reshape(N_GX * N_GY, N_GZ, TABLE, COMPS, RH)
    root_keys = jax.vmap(lambda grid_col, slab_here: lax.dynamic_index_in_dim(grid_col, slab_here, axis=0, keepdims=False))(root_grid, slab_index)
    pvec_dev = jnp.transpose(probe_vectors.reshape(3, KP, devices, P_DEV), (2, 0, 1, 3))
    pidx_dev = jnp.transpose(probe_index.reshape(KP, devices, P_DEV), (1, 0, 2))
    pcnt_dev = probe_count.reshape(devices, P_DEV)

    def probe_device(items):
        device, vector_part, index_part, count_part = items
        key_rows = lax.dynamic_index_in_dim(root_keys, device // N_GZ, axis=0, keepdims=False)
        return probe_rows(key_rows, vector_part, index_part, count_part, probe_in, probe_mid)
    density = lax.map(probe_device, (jnp.arange(devices, dtype=jnp.int32), pvec_dev, pidx_dev, pcnt_dev))
    return (atom_features, density.reshape(PROBES))
```

```python
import functools
import math

import jax
import jax.numpy as jnp
import numpy as np
from jax import lax
from jax.experimental import pallas as pl
from jax.experimental.pallas import tpu as pltpu
from jax.sharding import PartitionSpec as P

C = 96
COMPS = 16
WIDTH = C * COMPS
RH = 64
NB = 8
K = 32
LAYERS = 3
ATOMS = 128
FACE = 32
GHOSTS = 192
TABLE = 320
HALF = 64
CUTOFF = 4.0
DEGREE = (0, 1, 1, 1, 2, 2, 2, 2, 2, 3, 3, 3, 3, 3, 3, 3)
STARTS = (0, 1, 4, 9)
WIDTHS = (1, 3, 5, 7)
STEP = 2
PAIRS = K // (2 * STEP)
WIDE = 4
STEPS = K // WIDE
ENV_ROW = 16
BASIS_ROW = 24
GEO_ROWS = 32

VMEM_LIMIT = 24 * 1024 * 1024

f32 = jnp.float32
bf16 = jnp.bfloat16


def dot(a, b):
    return lax.dot_general(a, b, (((1,), (0,)), ((), ())), preferred_element_type=f32)


def dot_tn(a, b):
    return lax.dot_general(a, b, (((0,), (0,)), ((), ())), preferred_element_type=f32)


def dot_nt(a, b):
    return lax.dot_general(a, b, (((1,), (1,)), ((), ())), preferred_element_type=f32)


def sigmoid(u):
    return 0.5 * jnp.tanh(0.5 * u) + 0.5


def silu(u):
    half = 0.5 * u
    return half * jnp.tanh(half) + half


def harmonics(vx, vy, vz):
    x = vx * 0.5
    y = vy * 0.5
    z = vz * 0.5
    q = x * x + y * y + z * z
    zz = 5.0 * z * z - q
    return [
        jnp.ones_like(x),
        math.sqrt(3.0) * x,
        math.sqrt(3.0) * y,
        math.sqrt(3.0) * z,
        math.sqrt(15.0) * x * y,
        math.sqrt(15.0) * y * z,
        math.sqrt(5.0) / 2.0 * (3.0 * z * z - q),
        math.sqrt(15.0) * x * z,
        math.sqrt(15.0) / 2.0 * (x * x - y * y),
        math.sqrt(35.0 / 8.0) * y * (3.0 * x * x - y * y),
        math.sqrt(105.0) * x * y * z,
        math.sqrt(21.0 / 8.0) * y * zz,
        math.sqrt(7.0) / 2.0 * z * (5.0 * z * z - 3.0 * q),
        math.sqrt(21.0 / 8.0) * x * zz,
        math.sqrt(105.0) / 2.0 * z * (x * x - y * y),
        math.sqrt(35.0 / 8.0) * x * (x * x - 3.0 * y * y),
    ]


def params(semantics=None):
    return pltpu.CompilerParams(vmem_limit_bytes=VMEM_LIMIT, dimension_semantics=semantics)


def whole(*shape):
    return pl.BlockSpec(shape, lambda i: (0,) * len(shape))


def layer_block(t, *shape):
    return pl.BlockSpec((None,) + shape, lambda i: (t,) + (0,) * len(shape))


def slots(*shape):
    return pl.BlockSpec((WIDE,) + shape, lambda i: (i,) + (0,) * len(shape))


def pick_kernel(lists_ref, rows_ref, sel_ref, *out_refs):
    lists = jnp.concatenate(
        [lists_ref[i, j, k : k + 1, :] for i in (0, 1) for j in (0, 1) for k in (0, 1)], axis=0
    )
    entry = lax.broadcasted_iota(jnp.int32, (8, GHOSTS), 0)
    lane = lax.broadcasted_iota(jnp.int32, (8, GHOSTS), 1)
    spread = dot(lists.astype(f32).astype(bf16), (entry == lane % 8).astype(f32).astype(bf16))
    face, quarter = lane // FACE, (lane // 8) % 4
    side = 1 - face % 2
    high, low = quarter // 2, quarter % 2
    octant = jnp.where(
        face < 2, 4 * side + quarter, jnp.where(face < 4, 4 * high + 2 * side + low, 2 * quarter + side)
    )
    chosen = jnp.sum(jnp.where(entry == octant, spread, 0.0), axis=0, keepdims=True)
    atom = lax.broadcasted_iota(jnp.int32, (ATOMS, GHOSTS), 0)
    turned_sel = (atom == chosen.astype(jnp.int32)).astype(f32)
    sel = turned_sel.T.astype(bf16)
    sel_ref[...] = sel
    picked = dot(sel, rows_ref[...]).astype(bf16)
    for number, out_ref in enumerate(out_refs):
        out_ref[...] = picked[number * FACE : (number + 1) * FACE]


def pick(lists, rows):
    return pl.pallas_call(
        pick_kernel,
        grid=(1,),
        in_specs=[whole(2, 2, 2, 8), whole(ATOMS, WIDTH)],
        out_specs=[whole(GHOSTS, ATOMS)] + [whole(FACE, WIDTH)] * 6,
        out_shape=[jax.ShapeDtypeStruct((GHOSTS, ATOMS), bf16)]
        + [jax.ShapeDtypeStruct((FACE, WIDTH), bf16)] * 6,
        compiler_params=params(),
        name="pick",
    )(lists, rows)


def geometry_into(vec_ref, count_ref, geo_ref):
    sharpness = ((NB - 1) / CUTOFF) ** 2
    centers = lax.broadcasted_iota(jnp.int32, (NB, ATOMS), 0).astype(f32) * (CUTOFF / (NB - 1))

    def one_slot(k, carry):
        vx = vec_ref[0, pl.ds(k, 1), :]
        vy = vec_ref[1, pl.ds(k, 1), :]
        vz = vec_ref[2, pl.ds(k, 1), :]
        square = vx * vx + vy * vy + vz * vz
        shape = 1.0 - square / (CUTOFF * CUTOFF)
        valid = (k < count_ref[...]).astype(f32)
        envelope = shape * shape * valid * (K ** (-0.5))
        radius = jnp.sqrt(square)
        offset = radius - centers
        for m, value in enumerate(harmonics(vx, vy, vz)):
            geo_ref[k, m : m + 1, :] = value
        geo_ref[k, ENV_ROW:BASIS_ROW, :] = jnp.broadcast_to(envelope, (8, ATOMS))
        geo_ref[k, BASIS_ROW:GEO_ROWS, :] = jnp.exp(-sharpness * offset * offset)
        return carry

    lax.fori_loop(0, K, one_slot, 0, unroll=4)


def prepare_kernel(rows_ref, avec_ref, acount_ref, pvec_ref, pcount_ref, turned_ref, ageo_ref, pgeo_ref):
    turned_ref[...] = rows_ref[...].astype(f32).T.astype(bf16)
    geometry_into(avec_ref, acount_ref, ageo_ref)
    geometry_into(pvec_ref, pcount_ref, pgeo_ref)


def prepare(rows, avec, acount, pvec, pcount):
    geo = jax.ShapeDtypeStruct((K, GEO_ROWS, ATOMS), f32)
    return pl.pallas_call(
        prepare_kernel,
        grid=(1,),
        in_specs=[
            whole(ATOMS, WIDTH),
            whole(3, K, ATOMS),
            whole(1, ATOMS),
            whole(3, K, ATOMS),
            whole(1, ATOMS),
        ],
        out_specs=[whole(WIDTH, ATOMS), whole(K, GEO_ROWS, ATOMS), whole(K, GEO_ROWS, ATOMS)],
        out_shape=[jax.ShapeDtypeStruct((WIDTH, ATOMS), bf16), geo, geo],
        compiler_params=params(),
        cost_estimate=pl.CostEstimate(flops=10_000_000, bytes_accessed=3_000_000, transcendentals=100_000),
        name="prepare",
    )(rows, avec, acount, pvec, pcount)


def hidden_kernel(species_ref, geo_ref, win_ref, wemb_ref, wmid_ref, out_ref):
    ids = lax.broadcasted_iota(jnp.int32, (wemb_ref.shape[1], ATOMS), 0)
    emb = dot(wemb_ref[...], (ids == species_ref[...]).astype(f32).astype(bf16))
    for k in range(0, K, 8):
        basis = jnp.concatenate([geo_ref[k + s, BASIS_ROW:GEO_ROWS, :] for s in range(8)], axis=1)
        hidden = dot_tn(win_ref[...], basis.astype(bf16)) + jnp.concatenate([emb] * 8, axis=1)
        hidden = silu(hidden).astype(bf16)
        hidden = silu(dot_tn(wmid_ref[...], hidden)).astype(bf16)
        for s in range(8):
            out_ref[k + s] = hidden[:, s * ATOMS : (s + 1) * ATOMS]


def hidden_units(t, species, geo, radial_in, species_emb, radial_mid):
    return pl.pallas_call(
        hidden_kernel,
        grid=(1,),
        in_specs=[
            whole(1, ATOMS),
            whole(K, GEO_ROWS, ATOMS),
            layer_block(t, NB, RH),
            layer_block(t, RH, species_emb.shape[2]),
            layer_block(t, RH, RH),
        ],
        out_specs=whole(K, RH, ATOMS),
        out_shape=jax.ShapeDtypeStruct((K, RH, ATOMS), bf16),
        compiler_params=params(),
        cost_estimate=pl.CostEstimate(
            flops=2 * 4096 * 256 * RH * 2, bytes_accessed=2_000_000, transcendentals=600_000
        ),
        name="hidden_units",
    )(species, geo, radial_in, species_emb, radial_mid)


def layer_kernel(last, *refs):
    (idx_ref, geo_ref, hidden_ref, turned_ref, sel_ref, wout_ref, mix_ref, gate_ref, proj_ref) = refs[:9]
    ghost_refs = refs[9:15]
    out_refs = refs[15:-5]
    table_ref, acc_ref, even_ref, odd_ref, rad_ref = refs[-5:]

    table_ref[:, :ATOMS] = turned_ref[...]
    rows = jnp.concatenate([ref[...] for ref in ghost_refs], axis=0)
    table_ref[:, ATOMS:] = rows.astype(f32).T.astype(bf16)

    def front(first, got_ref, slot):
        hidden = jnp.concatenate([hidden_ref[first + s] for s in range(STEP)], axis=1)
        envelope = jnp.concatenate(
            [geo_ref[first + s, ENV_ROW : ENV_ROW + 1, :] for s in range(STEP)], axis=1
        )
        rad_ref[slot] = dot_tn(wout_ref[...], hidden) * envelope
        ids = lax.broadcasted_iota(jnp.int32, (TABLE, ATOMS), 0)
        hot = jnp.concatenate(
            [
                (ids == idx_ref[pl.ds(first + s, 1), :]).astype(f32).astype(bf16)
                for s in range(STEP)
            ],
            axis=1,
        )
        got_ref[...] = dot(table_ref[...], hot)

    def back(first, got_ref, slot, keep):
        for tile in range(0, C, 8):
            scalar = []
            weight = []
            for s in range(STEP):
                lanes = slice(s * ATOMS, (s + 1) * ATOMS)
                scalar.append(got_ref[tile : tile + 8, lanes])
                weight.append(
                    [rad_ref[slot, l * C + tile : l * C + tile + 8, lanes] for l in range(4)]
                )
            for m in range(COMPS):
                at = m * C + tile
                total = acc_ref[at : at + 8, :]
                for s in range(STEP):
                    if m == 0:
                        value = scalar[s]
                    else:
                        value = got_ref[at : at + 8, s * ATOMS : (s + 1) * ATOMS]
                        value = value + geo_ref[first + s, m : m + 1, :] * scalar[s]
                    total = total + weight[s][DEGREE[m]] * value
                acc_ref[at : at + 8, :] = total if keep is None else jnp.where(keep, total, 0.0)

    def two_steps(i, carry):
        first = i * (2 * STEP)
        front(first, even_ref, 0)
        back(jnp.maximum(first - STEP, 0), odd_ref, 1, i > 0)
        front(first + STEP, odd_ref, 1)
        back(first, even_ref, 0, None)
        return carry

    lax.fori_loop(0, PAIRS, two_steps, 0)
    back(K - STEP, odd_ref, 1, None)

    message = [acc_ref[m * C : (m + 1) * C, :].astype(bf16) for m in range(COMPS)]
    gate = sigmoid(dot_tn(gate_ref[...], message[0]))
    updated = []
    for degree in range(4):
        start, width = STARTS[degree], WIDTHS[degree]
        mixed = dot_tn(mix_ref[degree], jnp.concatenate(message[start : start + width], axis=1))
        for j in range(width):
            m = start + j
            part = mixed[:, j * ATOMS : (j + 1) * ATOMS]
            before = turned_ref[m * C : (m + 1) * C, :].astype(f32)
            change = silu(part) if degree == 0 else gate * part
            updated.append((before + change).astype(bf16))
    new = jnp.concatenate(updated, axis=0)
    sel = sel_ref[...]
    if not last:
        out_refs[0][...] = new
        picked = dot_nt(sel, new).astype(bf16)
        for face in range(6):
            out_refs[1 + face][...] = picked[face * FACE : (face + 1) * FACE]
    else:
        ones = (
            lax.broadcasted_iota(jnp.int32, (ATOMS, ATOMS), 0)
            == lax.broadcasted_iota(jnp.int32, (ATOMS, ATOMS), 1)
        ).astype(f32).astype(bf16)
        out_refs[0][...] = dot_nt(ones, new).astype(bf16)
        keys = jnp.concatenate(
            [dot(proj_ref[DEGREE[m]], updated[m]) for m in range(COMPS)], axis=0
        ).astype(bf16)
        rows = dot_nt(jnp.concatenate([sel, ones], axis=0), keys).astype(bf16)
        for face in range(6):
            out_refs[1 + face][...] = rows[face * FACE : (face + 1) * FACE]
        out_refs[7][...] = rows[GHOSTS : GHOSTS + HALF]
        out_refs[8][...] = rows[GHOSTS + HALF :]


def layer(t, idx, geo, hidden, turned, sel, ghosts, weights):
    last = t == LAYERS - 1
    if last:
        shapes = [(ATOMS, WIDTH)] + [(FACE, COMPS * RH)] * 6 + [(HALF, COMPS * RH)] * 2
    else:
        shapes = [(WIDTH, ATOMS)] + [(FACE, WIDTH)] * 6
    lanes = STEP * ATOMS
    return pl.pallas_call(
        functools.partial(layer_kernel, last),
        grid=(1,),
        in_specs=[
            whole(K, ATOMS),
            whole(K, GEO_ROWS, ATOMS),
            whole(K, RH, ATOMS),
            whole(WIDTH, ATOMS),
            whole(GHOSTS, ATOMS),
            layer_block(t, RH, 4 * C),
            layer_block(t, 4, C, C),
            layer_block(t, C, C),
            whole(4, RH, C),
        ]
        + [whole(FACE, WIDTH)] * 6,
        out_specs=[whole(*shape) for shape in shapes],
        out_shape=[jax.ShapeDtypeStruct(shape, bf16) for shape in shapes],
        scratch_shapes=[
            pltpu.VMEM((WIDTH, TABLE), bf16),
            pltpu.VMEM((WIDTH, ATOMS), f32),
            pltpu.VMEM((WIDTH, lanes), f32),
            pltpu.VMEM((WIDTH, lanes), f32),
            pltpu.VMEM((2, 4 * C, lanes), f32),
        ],
        compiler_params=params(),
        cost_estimate=pl.CostEstimate(
            flops=2 * 4096 * 512 * WIDTH, bytes_accessed=3_000_000, transcendentals=600_000
        ),
        name="layer",
    )(idx, geo, hidden, turned, sel, *weights, *ghosts)


def probe_weights_kernel(geo_ref, win_ref, wmid_ref, out_ref):
    basis = jnp.concatenate([geo_ref[s, BASIS_ROW:GEO_ROWS, :] for s in range(WIDE)], axis=1)
    hidden = silu(dot_tn(win_ref[...], basis.astype(bf16))).astype(bf16)
    hidden = silu(dot_tn(wmid_ref[...], hidden)).astype(bf16).astype(f32)
    for s in range(WIDE):
        scaled = hidden[:, s * ATOMS : (s + 1) * ATOMS] * geo_ref[s, ENV_ROW : ENV_ROW + 1, :]
        for m in range(COMPS):
            value = scaled if m == 0 else scaled * geo_ref[s, m : m + 1, :]
            out_ref[s, m * RH : (m + 1) * RH, :] = value.astype(bf16)


def probe_weights(geo, probe_in, probe_mid):
    return pl.pallas_call(
        probe_weights_kernel,
        grid=(STEPS,),
        in_specs=[slots(GEO_ROWS, ATOMS), whole(NB, RH), whole(RH, RH)],
        out_specs=slots(COMPS * RH, ATOMS),
        out_shape=jax.ShapeDtypeStruct((K, COMPS * RH, ATOMS), bf16),
        compiler_params=params(("arbitrary",)),
        cost_estimate=pl.CostEstimate(
            flops=2 * 4096 * 256 * WIDTH, bytes_accessed=9_000_000, transcendentals=600_000
        ),
        name="probe_weights",
    )(geo, probe_in, probe_mid)


def readout_kernel(place_ref, idx_ref, weight_ref, near_ref, far_ref, out_ref, keys_ref, acc_ref):
    step = pl.program_id(0)

    @pl.when(step == 0)
    def _():
        chip, core, root_chip, root_core = [place_ref[j] for j in range(4)]
        both = jnp.where(core == root_core, 1, 0)

        def fetch(at, rows, offset, other):
            start = pl.multiple_of(lax.rem(chip - root_chip - offset + 8, 4) * HALF, HALF)
            same = both if other == 0 else 1 - both

            @pl.when(same == 1)
            def _():
                keys_ref[at : at + rows, :] = near_ref[pl.ds(start, rows), :]

            @pl.when(same == 0)
            def _():
                keys_ref[at : at + rows, :] = far_ref[pl.ds(start, rows), :]

        fetch(0, HALF, 0, 0)
        fetch(HALF, HALF, 0, 1)
        for face, (offset, other) in enumerate(HOLDERS):
            fetch(ATOMS + face * FACE, FACE, offset, other)
        acc_ref[...] = jnp.zeros_like(acc_ref)

    weight = jnp.concatenate([weight_ref[s] for s in range(WIDE)], axis=1)
    product = dot(keys_ref[...], weight)
    rows = lax.broadcasted_iota(jnp.int32, (TABLE, ATOMS), 0)
    total = acc_ref[...]
    for s in range(WIDE):
        chosen = rows == idx_ref[pl.ds(step * WIDE + s, 1), :]
        part = jnp.where(chosen, product[:, s * ATOMS : (s + 1) * ATOMS], 0.0)
        total = total + jnp.sum(part.reshape(TABLE // 8, 8, ATOMS), axis=0)
    acc_ref[...] = total

    @pl.when(step == STEPS - 1)
    def _():
        out_ref[...] = jnp.sum(acc_ref[...], axis=0, keepdims=True)


def readout(place, idx, weight, near, far):
    return pl.pallas_call(
        readout_kernel,
        grid_spec=pltpu.PrefetchScalarGridSpec(
            num_scalar_prefetch=1,
            grid=(STEPS,),
            in_specs=[
                pl.BlockSpec((K, ATOMS), lambda i, place: (0, 0)),
                pl.BlockSpec((WIDE, COMPS * RH, ATOMS), lambda i, place: (i, 0, 0)),
                pl.BlockSpec((4 * HALF, COMPS * RH), lambda i, place: (0, 0)),
                pl.BlockSpec((4 * HALF, COMPS * RH), lambda i, place: (0, 0)),
            ],
            out_specs=pl.BlockSpec((1, ATOMS), lambda i, place: (0, 0)),
            scratch_shapes=[pltpu.VMEM((TABLE, COMPS * RH), bf16), pltpu.VMEM((8, ATOMS), f32)],
        ),
        out_shape=jax.ShapeDtypeStruct((1, ATOMS), f32),
        compiler_params=params(("arbitrary",)),
        name="readout",
    )(place, idx, weight, near, far)


DIRECTIONS = (("gx", 1), ("gx", -1), ("gy", 1), ("gy", -1), ("gz", 1), ("gz", -1))
HOLDERS = ((1, 0), (3, 0), (2, 0), (2, 1), (3, 1), (1, 1))
SENT_FIRST = (2, 3, 0, 1, 4, 5)


def shift(block, axis, by):
    count = lax.axis_size(axis)
    return lax.ppermute(block, axis, [(i, (i + by) % count) for i in range(count)])


def exchange(faces):
    landed = [None] * 6
    for face in SENT_FIRST:
        axis, by = DIRECTIONS[face]
        landed[face] = shift(faces[face], axis, by)
    return landed


def holder(place, offset, other):
    return (place // 2 + offset) % 4 * 2 + (place % 2 + other) % 2


def to_holder(block, axis, by, offset, other):
    outer, inner = lax.axis_size(axis), lax.axis_size("gz")
    if axis == "gz":
        pairs = [(i, holder((i + by) % inner, offset, other)) for i in range(inner)]
        return lax.ppermute(block, axis, pairs)
    pairs = [
        (i * inner + j, (i + by) % outer * inner + holder(j, offset, other))
        for i in range(outer)
        for j in range(inner)
    ]
    return lax.ppermute(block, (axis, "gz"), pairs)


def column_keys(faces, own_low, own_high, chip, core, root_chip, root_core, probe_weight):
    landed = [None] * 6
    for face in SENT_FIRST:
        landed[face] = to_holder(faces[face], *DIRECTIONS[face], *HOLDERS[face])
    other_half = to_holder(own_high, "gz", 0, 0, 1)
    offset = (chip - root_chip + 4) % 4
    other = (core - root_core + 2) % 2
    at_root = (offset == 0) & (other == 0)
    low = jnp.where(at_root, own_low[:FACE], other_half[:FACE])
    for face in range(6):
        here = (offset == HOLDERS[face][0]) & (other == HOLDERS[face][1])
        low = jnp.where(here, landed[face], low)
    high = jnp.where(at_root, own_low[FACE:], other_half[FACE:])
    mine = jnp.concatenate([low, high], axis=0)
    moved = [
        lax.ppermute(mine, "gz", [(i, (i + 2 * by) % 8) for i in range(8)]) for by in (1, 2, 3)
    ]
    *moved, probe_weight = lax.optimization_barrier((*moved, probe_weight))
    near = jnp.concatenate([mine] + moved, axis=0)
    far = lax.ppermute(near, "gz", [(i, i + 1 - 2 * (i % 2)) for i in range(8)])
    return near, far, probe_weight


def local(
    features,
    species,
    octant_lists,
    neighbour_index,
    neighbour_count,
    edge_vectors,
    radial_in,
    species_emb,
    radial_mid,
    radial_out,
    mix_weight,
    gate_weight,
    probe_in,
    probe_mid,
    probe_proj,
    probe_vectors,
    probe_index,
    probe_count,
    slab_index,
):
    column = lax.axis_index("gx") * lax.axis_size("gy") + lax.axis_index("gy")
    root = lax.dynamic_index_in_dim(slab_index, column, 0, keepdims=False)
    mine = lax.axis_index("gz")
    chip, core, root_chip, root_core = mine // 2, mine % 2, root // 2, root % 2

    sel, *faces = pick(octant_lists, features)
    ghosts = exchange(faces)
    turned, geo, probe_geo = prepare(
        features,
        edge_vectors,
        neighbour_count.reshape(1, ATOMS),
        probe_vectors,
        probe_count.reshape(1, ATOMS),
    )
    species_row = species.reshape(1, ATOMS)
    weights = (radial_out, mix_weight, gate_weight, jnp.swapaxes(probe_proj, 1, 2))
    emb_turned = jnp.swapaxes(species_emb, 1, 2)
    for t in range(LAYERS):
        hidden = hidden_units(t, species_row, geo, radial_in, emb_turned, radial_mid)
        outs = layer(t, neighbour_index, geo, hidden, turned, sel, ghosts, weights)
        if t < LAYERS - 1:
            turned = outs[0]
            ghosts = exchange(outs[1:])
    near, far, probe_weight = column_keys(
        outs[1:7], outs[7], outs[8], chip, core, root_chip, root_core,
        probe_weights(probe_geo, probe_in, probe_mid),
    )
    place = jnp.stack([chip, core, root_chip, root_core])
    density = readout(place, probe_index, probe_weight, near, far)
    return (outs[0], density.reshape(ATOMS))


def solution(mesh):
    in_specs = (
        P(("gx", "gy", "gz"), None),
        P(("gx", "gy", "gz")),
        P(None, None, None, ("gx", "gy", "gz")),
        P(None, ("gx", "gy", "gz")),
        P(("gx", "gy", "gz")),
        P(None, None, ("gx", "gy", "gz")),
        P(),
        P(),
        P(),
        P(),
        P(),
        P(),
        P(),
        P(),
        P(),
        P(None, None, ("gx", "gy", "gz")),
        P(None, ("gx", "gy", "gz")),
        P(("gx", "gy", "gz")),
        P(),
    )
    out_specs = (P(("gx", "gy", "gz"), None), P(("gx", "gy", "gz")))
    return jax.shard_map(local, mesh=mesh, in_specs=in_specs, out_specs=out_specs, check_vma=False)
```

```python
import functools
import math

import jax
import jax.numpy as jnp
import numpy as np
from jax import lax
from jax.experimental import pallas as pl
from jax.experimental.pallas import tpu as pltpu
from jax.sharding import PartitionSpec as P

C = 96
COMPS = 16
WIDTH = C * COMPS
RH = 64
NB = 8
SPECIES = 89
K = 32
LAYERS = 3
ATOMS = 128
FACE = 32
GHOSTS = 192
TABLE = 320
PADDED = 384
HALF = 64
CUTOFF = 4.0
DEGREE = (0, 1, 1, 1, 2, 2, 2, 2, 2, 3, 3, 3, 3, 3, 3, 3)
STARTS = (0, 1, 4, 9)
WIDTHS = (1, 3, 5, 7)
STEP = 2
PAIRS = K // (2 * STEP)
PARTS = 3
WIDE = 16
STEPS = K // WIDE
ENV_ROW = 16
BASIS_ROW = 24
GEO_ROWS = 32

VMEM_LIMIT = 24 * 1024 * 1024
VMEM_MOST = 62 * 1024 * 1024

f32 = jnp.float32
bf16 = jnp.bfloat16
f8 = jnp.float8_e4m3fn


def dot(a, b):
    return lax.dot_general(a, b, (((1,), (0,)), ((), ())), preferred_element_type=f32)


def dot_tn(a, b):
    return lax.dot_general(a, b, (((0,), (0,)), ((), ())), preferred_element_type=f32)


def dot_nt(a, b):
    return lax.dot_general(a, b, (((1,), (1,)), ((), ())), preferred_element_type=f32)


def sigmoid(u):
    return 0.5 * jnp.tanh(0.5 * u) + 0.5


def silu(u):
    half = 0.5 * u
    return half * jnp.tanh(half) + half


def power_scale(largest):
    scale = jnp.ones_like(largest)
    inverse = jnp.ones_like(largest)
    for j in (64, 32, 16, 8, 4, 2, 1):
        up = largest * inverse > 224.0 * 2.0**j
        scale = jnp.where(up, scale * 2.0**j, scale)
        inverse = jnp.where(up, inverse * 2.0**-j, inverse)
    for j in (32, 16, 8, 4, 2, 1):
        down = largest * inverse * 2.0**j <= 448.0
        scale = jnp.where(down, scale * 2.0**-j, scale)
        inverse = jnp.where(down, inverse * 2.0**j, inverse)
    return scale, inverse


def harmonics(vx, vy, vz):
    x = vx * 0.5
    y = vy * 0.5
    z = vz * 0.5
    q = x * x + y * y + z * z
    zz = 5.0 * z * z - q
    return [
        jnp.ones_like(x),
        math.sqrt(3.0) * x,
        math.sqrt(3.0) * y,
        math.sqrt(3.0) * z,
        math.sqrt(15.0) * x * y,
        math.sqrt(15.0) * y * z,
        math.sqrt(5.0) / 2.0 * (3.0 * z * z - q),
        math.sqrt(15.0) * x * z,
        math.sqrt(15.0) / 2.0 * (x * x - y * y),
        math.sqrt(35.0 / 8.0) * y * (3.0 * x * x - y * y),
        math.sqrt(105.0) * x * y * z,
        math.sqrt(21.0 / 8.0) * y * zz,
        math.sqrt(7.0) / 2.0 * z * (5.0 * z * z - 3.0 * q),
        math.sqrt(21.0 / 8.0) * x * zz,
        math.sqrt(105.0) / 2.0 * z * (x * x - y * y),
        math.sqrt(35.0 / 8.0) * x * (x * x - 3.0 * y * y),
    ]


def params(semantics=None, limit=VMEM_LIMIT):
    return pltpu.CompilerParams(vmem_limit_bytes=limit, dimension_semantics=semantics)


def whole(*shape):
    return pl.BlockSpec(shape, lambda i: (0,) * len(shape))


def slots(*shape):
    return pl.BlockSpec((WIDE,) + shape, lambda i: (i,) + (0,) * len(shape))


def in_vmem(count):
    return [pl.BlockSpec(memory_space=pltpu.VMEM)] * count


def in_hbm(count):
    return [pl.BlockSpec(memory_space=pltpu.HBM)] * count


def like(array):
    return jax.ShapeDtypeStruct(array.shape, array.dtype)


AXES = ("gx", "gy", "gz")
BLOCKS = 6
SENT = (3, 5, 2, 0, 1, 4)


def partner(index, count, turn):
    return (index + 1) % count if index % 2 == turn else (index - 1) % count


def parity(axis_number):
    return lax.axis_index(AXES[axis_number]) % 2


def pick_kernel(lists_hbm, rows_hbm, sel_ref, *refs):
    out_refs = refs[:BLOCKS]
    lists_ref, rows_ref, sems = refs[BLOCKS:]
    rows_copy = pltpu.make_async_copy(rows_hbm, rows_ref, sems.at[0])
    rows_copy.start()
    lists_copy = pltpu.make_async_copy(lists_hbm, lists_ref, sems.at[1])
    lists_copy.start()
    lists_copy.wait()
    lists = jnp.concatenate(
        [lists_ref[i, j, k : k + 1, :] for i in (0, 1) for j in (0, 1) for k in (0, 1)], axis=0
    )
    entry = lax.broadcasted_iota(jnp.int32, (8, GHOSTS), 0)
    lane = lax.broadcasted_iota(jnp.int32, (8, GHOSTS), 1)
    spread = dot(lists.astype(f32).astype(bf16), (entry == lane % 8).astype(f32).astype(bf16))
    block, quarter = lane // FACE, (lane // 8) % 4
    odd = jnp.where(block < 2, parity(0), jnp.where(block < 4, parity(1), parity(2)))
    side = jnp.where(block % 2 == odd, 1, 0)
    high, low = quarter // 2, quarter % 2
    octant = jnp.where(
        block < 2, 4 * side + quarter, jnp.where(block < 4, 4 * high + 2 * side + low, 2 * quarter + side)
    )
    chosen = jnp.sum(jnp.where(entry == octant, spread, 0.0), axis=0, keepdims=True)
    atom = lax.broadcasted_iota(jnp.int32, (ATOMS, GHOSTS), 0)
    turned_sel = (atom == chosen.astype(jnp.int32)).astype(f32)
    sel = turned_sel.T.astype(bf16)
    sel_ref[...] = sel
    rows_copy.wait()
    picked = dot(sel, rows_ref[...]).astype(bf16)
    for number, out_ref in enumerate(out_refs):
        out_ref[...] = picked[number * FACE : (number + 1) * FACE]


def pick(lists, rows):
    return pl.pallas_call(
        pick_kernel,
        grid=(1,),
        in_specs=in_hbm(2),
        out_specs=[whole(GHOSTS, ATOMS)] + [whole(FACE, WIDTH)] * BLOCKS,
        out_shape=[jax.ShapeDtypeStruct((GHOSTS, ATOMS), bf16)]
        + [jax.ShapeDtypeStruct((FACE, WIDTH), bf16)] * BLOCKS,
        scratch_shapes=[
            pltpu.VMEM(lists.shape, jnp.int32),
            pltpu.VMEM(rows.shape, bf16),
            pltpu.SemaphoreType.DMA((2,)),
        ],
        compiler_params=params(),
        name="pick",
    )(lists, rows)


def geometry_into(vec_ref, count_ref, geo_ref):
    sharpness = ((NB - 1) / CUTOFF) ** 2
    centers = lax.broadcasted_iota(jnp.int32, (NB, ATOMS), 0).astype(f32) * (CUTOFF / (NB - 1))

    def one_slot(k, carry):
        vx = vec_ref[0, pl.ds(k, 1), :]
        vy = vec_ref[1, pl.ds(k, 1), :]
        vz = vec_ref[2, pl.ds(k, 1), :]
        square = vx * vx + vy * vy + vz * vz
        shape = 1.0 - square / (CUTOFF * CUTOFF)
        valid = (k < count_ref[...]).astype(f32)
        envelope = shape * shape * valid * (K ** (-0.5))
        radius = jnp.sqrt(square)
        offset = radius - centers
        for m, value in enumerate(harmonics(vx, vy, vz)):
            geo_ref[k, m : m + 1, :] = value
        geo_ref[k, ENV_ROW:BASIS_ROW, :] = jnp.broadcast_to(envelope, (8, ATOMS))
        geo_ref[k, BASIS_ROW:GEO_ROWS, :] = jnp.exp(-sharpness * offset * offset)
        return carry

    lax.fori_loop(0, K, one_slot, 0, unroll=4)


PACK_OUT = 0
PACK_MIX = 192
PACK_GATE = 576
PACK_MID = 672
PACK_EMB = 736
PACK_IN = 800
PACK_LAYER = 816
PACK_PROJ = LAYERS * PACK_LAYER
PACK_PROBE_IN = PACK_PROJ + 256
PACK_PROBE_MID = PACK_PROBE_IN + 16
PACK_ROWS = PACK_PROBE_MID + 64
WEIGHTS = 9


def pack_weights(refs, pack_ref):
    win_ref, wemb_ref, wmid_ref, wout_ref, mix_ref, gate_ref, proj_ref, pin_ref, pmid_ref = refs

    def put(at, value):
        pack_ref[at : at + value.shape[0], : value.shape[1]] = value

    def padded(value):
        return jnp.concatenate([value, jnp.zeros_like(value)], axis=0)

    for t in range(LAYERS):
        base = t * PACK_LAYER
        for j in range(3):
            put(base + PACK_OUT + RH * j, wout_ref[t, :, 128 * j : 128 * (j + 1)])
        for degree in range(4):
            put(base + PACK_MIX + C * degree, mix_ref[t, degree])
        put(base + PACK_GATE, gate_ref[t])
        put(base + PACK_MID, wmid_ref[t])
        put(base + PACK_EMB, wemb_ref[t])
        put(base + PACK_IN, padded(win_ref[t]))
    for degree in range(4):
        put(PACK_PROJ + RH * degree, proj_ref[degree])
    put(PACK_PROBE_IN, padded(pin_ref[...]))
    put(PACK_PROBE_MID, pmid_ref[...])


def hidden_into(t, species_ref, geo_ref, pack_ref, out_ref):
    base = t * PACK_LAYER
    wemb = pack_ref[base + PACK_EMB : base + PACK_EMB + RH, :SPECIES]
    win = pack_ref[base + PACK_IN : base + PACK_IN + 16, :RH][:NB]
    wmid = pack_ref[base + PACK_MID : base + PACK_MID + RH, :RH]
    ids = lax.broadcasted_iota(jnp.int32, (SPECIES, ATOMS), 0)
    emb = dot(wemb, (ids == species_ref[...]).astype(f32).astype(bf16))
    for k in range(0, K, 8):
        basis = jnp.concatenate([geo_ref[k + s, BASIS_ROW:GEO_ROWS, :] for s in range(8)], axis=1)
        hidden = dot_tn(win, basis.astype(bf16)) + jnp.concatenate([emb] * 8, axis=1)
        hidden = silu(hidden).astype(bf16)
        hidden = silu(dot_tn(wmid, hidden)).astype(bf16)
        for s in range(8):
            out_ref[k + s] = hidden[:, s * ATOMS : (s + 1) * ATOMS]


def prepare_kernel(*refs):
    inputs = refs[: 7 + WEIGHTS]
    turned_ref, ageo_ref, pgeo_ref, index_ref, hidden_ref, pack_ref = refs[7 + WEIGHTS : 13 + WEIGHTS]
    *landed, sems = refs[13 + WEIGHTS :]
    copies = [
        pltpu.make_async_copy(source, target, sems.at[number])
        for number, (source, target) in enumerate(zip(inputs, landed))
    ]
    for copy in copies:
        copy.start()
    avec_ref, acount_ref, rows_ref, old_ref, pvec_ref, pcount_ref, species_ref = landed[:7]
    copies[0].wait()
    copies[1].wait()
    geometry_into(avec_ref, acount_ref, ageo_ref)
    copies[2].wait()
    turned_ref[...] = rows_ref[...].astype(f32).T.astype(bf16)
    copies[3].wait()
    index = old_ref[...]
    block = (index - ATOMS) // FACE
    odd = jnp.where(block < 2, parity(0), jnp.where(block < 4, parity(1), parity(2)))
    moved = jnp.where(block % 2 == 0, index + FACE, index - FACE)
    index_ref[...] = jnp.where((index >= ATOMS) & (odd == 0), moved, index)
    copies[4].wait()
    copies[5].wait()
    geometry_into(pvec_ref, pcount_ref, pgeo_ref)
    for copy in copies[6:]:
        copy.wait()
    pack_weights(landed[7:], pack_ref)
    hidden_into(0, species_ref, ageo_ref, pack_ref, hidden_ref)


def prepare(inputs):
    outs = [
        jax.ShapeDtypeStruct((WIDTH, ATOMS), bf16),
        jax.ShapeDtypeStruct((K, GEO_ROWS, ATOMS), f32),
        jax.ShapeDtypeStruct((K, GEO_ROWS, ATOMS), f32),
        jax.ShapeDtypeStruct((K, ATOMS), jnp.int32),
        jax.ShapeDtypeStruct((K, RH, ATOMS), bf16),
        jax.ShapeDtypeStruct((PACK_ROWS, 128), bf16),
    ]
    return pl.pallas_call(
        prepare_kernel,
        grid=(1,),
        in_specs=in_hbm(7 + WEIGHTS),
        out_specs=[whole(*out.shape) for out in outs],
        out_shape=outs,
        scratch_shapes=[pltpu.VMEM(array.shape, array.dtype) for array in inputs]
        + [pltpu.SemaphoreType.DMA((7 + WEIGHTS,))],
        compiler_params=params(limit=VMEM_MOST),
        cost_estimate=pl.CostEstimate(flops=10_000_000, bytes_accessed=9_000_000, transcendentals=100_000),
        name="prepare",
    )(*inputs)


def hidden_kernel(t, species_ref, geo_ref, pack_ref, out_ref):
    hidden_into(t, species_ref, geo_ref, pack_ref, out_ref)


def hidden_units(t, species, geo, pack):
    return pl.pallas_call(
        functools.partial(hidden_kernel, t),
        grid=(1,),
        in_specs=[whole(1, ATOMS), whole(K, GEO_ROWS, ATOMS), whole(PACK_ROWS, 128)],
        out_specs=whole(K, RH, ATOMS),
        out_shape=jax.ShapeDtypeStruct((K, RH, ATOMS), bf16),
        compiler_params=params(),
        cost_estimate=pl.CostEstimate(
            flops=2 * 4096 * 256 * RH * 2, bytes_accessed=2_000_000, transcendentals=600_000
        ),
        name="hidden_units",
    )(species, geo, pack)


def layer_kernel(t, *refs):
    last = t == LAYERS - 1
    base = t * PACK_LAYER
    idx_ref, geo_ref, hidden_ref, turned_ref, sel_ref, pack_ref = refs[:6]
    ghost_refs = refs[6:12]
    out_refs = refs[12:-5]
    wout = jnp.concatenate(
        [pack_ref[base + PACK_OUT + RH * j : base + PACK_OUT + RH * (j + 1), :] for j in range(3)],
        axis=1,
    )
    table_ref, acc_ref, even_ref, odd_ref, rad_ref = refs[-5:]

    own = turned_ref[...].astype(f32)
    ghosts = jnp.concatenate([ghost_refs[SENT.index(b)][...] for b in range(BLOCKS)], axis=0)
    ghosts = ghosts.astype(f32).T
    scale, inverse = power_scale(
        jnp.maximum(
            jnp.max(jnp.abs(own), axis=(0, 1), keepdims=True),
            jnp.max(jnp.abs(ghosts), axis=(0, 1), keepdims=True),
        )
    )
    for at, part in ((0, own), (ATOMS, ghosts)):
        lanes = part.shape[1]
        part = part * inverse
        high = part.astype(f8)
        table_ref[:, at : at + lanes] = high
        low = part - high.astype(f32)
        table_ref[:, PADDED + at : PADDED + at + lanes] = low.astype(f8)
    for at in (TABLE, PADDED + TABLE):
        table_ref[:, at : at + PADDED - TABLE] = jnp.zeros((WIDTH, PADDED - TABLE), f8)

    def front(first, slot):
        hidden = jnp.concatenate([hidden_ref[first + s] for s in range(STEP)], axis=1)
        envelope = jnp.concatenate(
            [geo_ref[first + s, ENV_ROW : ENV_ROW + 1, :] for s in range(STEP)], axis=1
        )
        rad_ref[slot] = dot_tn(wout, hidden) * (envelope * scale)
        ids = lax.broadcasted_iota(jnp.int32, (PADDED, ATOMS), 0)
        hot = jnp.concatenate(
            [(ids == idx_ref[pl.ds(first + s, 1), :]).astype(f32) for s in range(STEP)], axis=1
        )
        hot = hot.astype(f8)
        return jnp.concatenate([hot, hot], axis=0)

    def back(first, got_ref, slot, keep, tiles):
        for tile in tiles:
            scalar = []
            weight = []
            for s in range(STEP):
                lanes = slice(s * ATOMS, (s + 1) * ATOMS)
                scalar.append(got_ref[tile : tile + 8, lanes])
                weight.append(
                    [rad_ref[slot, l * C + tile : l * C + tile + 8, lanes] for l in range(4)]
                )
            for m in range(COMPS):
                at = m * C + tile
                total = acc_ref[at : at + 8, :]
                for s in range(STEP):
                    if m == 0:
                        value = scalar[s]
                    else:
                        value = got_ref[at : at + 8, s * ATOMS : (s + 1) * ATOMS]
                        value = value + geo_ref[first + s, m : m + 1, :] * scalar[s]
                    total = total + weight[s][DEGREE[m]] * value
                acc_ref[at : at + 8, :] = total if keep is None else jnp.where(keep, total, 0.0)

    def one_step(first, slot, behind, keep):
        got_ref, behind_ref = (even_ref, odd_ref) if slot == 0 else (odd_ref, even_ref)
        hot = front(first, slot)
        for part in range(PARTS):
            back(behind, behind_ref, 1 - slot, keep, range(part * C // PARTS, (part + 1) * C // PARTS, 8))
            rows = slice(part * WIDTH // PARTS, (part + 1) * WIDTH // PARTS)
            got_ref[rows, :] = dot(table_ref[rows, :], hot)

    def two_steps(i, carry):
        first = i * (2 * STEP)
        one_step(first, 0, jnp.maximum(first - STEP, 0), i > 0)
        one_step(first + STEP, 1, first, None)
        return carry

    lax.fori_loop(0, PAIRS, two_steps, 0)
    back(K - STEP, odd_ref, 1, None, range(0, C, 8))

    message = [acc_ref[m * C : (m + 1) * C, :].astype(bf16) for m in range(COMPS)]
    gate = sigmoid(dot_tn(pack_ref[base + PACK_GATE : base + PACK_GATE + C, :C], message[0]))
    updated = []
    for degree in range(4):
        start, width = STARTS[degree], WIDTHS[degree]
        at = base + PACK_MIX + C * degree
        mixed = dot_tn(pack_ref[at : at + C, :C], jnp.concatenate(message[start : start + width], axis=1))
        for j in range(width):
            m = start + j
            part = mixed[:, j * ATOMS : (j + 1) * ATOMS]
            before = turned_ref[m * C : (m + 1) * C, :].astype(f32)
            change = silu(part) if degree == 0 else gate * part
            updated.append((before + change).astype(bf16))
    new = jnp.concatenate(updated, axis=0)
    sel = sel_ref[...]
    if not last:
        out_refs[0][...] = new
        picked = dot_nt(sel, new).astype(bf16)
        for face in range(6):
            out_refs[1 + face][...] = picked[face * FACE : (face + 1) * FACE]
    else:
        ones = (
            lax.broadcasted_iota(jnp.int32, (ATOMS, ATOMS), 0)
            == lax.broadcasted_iota(jnp.int32, (ATOMS, ATOMS), 1)
        ).astype(f32).astype(bf16)
        out_refs[0][...] = dot_nt(ones, new).astype(bf16)
        keys = jnp.concatenate(
            [
                dot(pack_ref[PACK_PROJ + RH * l : PACK_PROJ + RH * (l + 1), :C], updated[m])
                for m, l in enumerate(DEGREE)
            ],
            axis=0,
        ).astype(bf16)
        rows = dot_nt(jnp.concatenate([sel, ones], axis=0), keys).astype(bf16)
        for face in range(6):
            out_refs[1 + face][...] = rows[face * FACE : (face + 1) * FACE]
        out_refs[7][...] = rows[GHOSTS : GHOSTS + HALF]
        out_refs[8][...] = rows[GHOSTS + HALF :]


def layer(t, idx, geo, hidden, turned, sel, ghosts, pack):
    last = t == LAYERS - 1
    if last:
        shapes = [(ATOMS, WIDTH)] + [(FACE, COMPS * RH)] * 6 + [(HALF, COMPS * RH)] * 2
    else:
        shapes = [(WIDTH, ATOMS)] + [(FACE, WIDTH)] * 6
    lanes = STEP * ATOMS
    return pl.pallas_call(
        functools.partial(layer_kernel, t),
        grid=(1,),
        in_specs=[
            whole(K, ATOMS),
            whole(K, GEO_ROWS, ATOMS),
            whole(K, RH, ATOMS),
            whole(WIDTH, ATOMS),
            whole(GHOSTS, ATOMS),
            whole(PACK_ROWS, 128),
        ]
        + [whole(FACE, WIDTH)] * BLOCKS,
        out_specs=[whole(*shape) for shape in shapes],
        out_shape=[jax.ShapeDtypeStruct(shape, bf16) for shape in shapes],
        scratch_shapes=[
            pltpu.VMEM((WIDTH, 2 * PADDED), f8),
            pltpu.VMEM((WIDTH, ATOMS), f32),
            pltpu.VMEM((WIDTH, lanes), f32),
            pltpu.VMEM((WIDTH, lanes), f32),
            pltpu.VMEM((2, 4 * C, lanes), f32),
        ],
        compiler_params=params(limit=VMEM_LIMIT),
        cost_estimate=pl.CostEstimate(
            flops=2 * 4096 * 512 * WIDTH, bytes_accessed=3_000_000, transcendentals=600_000
        ),
        name="layer",
    )(idx, geo, hidden, turned, sel, pack, *[ghosts[b] for b in SENT])


def probe_weights_kernel(geo_ref, pack_ref, out_ref):
    win = pack_ref[PACK_PROBE_IN : PACK_PROBE_IN + 16, :RH][:NB]
    wmid = pack_ref[PACK_PROBE_MID : PACK_PROBE_MID + RH, :RH]
    basis = jnp.concatenate([geo_ref[s, BASIS_ROW:GEO_ROWS, :] for s in range(WIDE)], axis=1)
    hidden = silu(dot_tn(win, basis.astype(bf16))).astype(bf16)
    hidden = silu(dot_tn(wmid, hidden)).astype(bf16).astype(f32)
    for s in range(WIDE):
        scaled = hidden[:, s * ATOMS : (s + 1) * ATOMS] * geo_ref[s, ENV_ROW : ENV_ROW + 1, :]
        for m in range(COMPS):
            value = scaled if m == 0 else scaled * geo_ref[s, m : m + 1, :]
            out_ref[s, m * RH : (m + 1) * RH, :] = value.astype(bf16)


def probe_weights(geo, pack):
    return pl.pallas_call(
        probe_weights_kernel,
        grid=(STEPS,),
        in_specs=[slots(GEO_ROWS, ATOMS), whole(PACK_ROWS, 128)],
        out_specs=slots(COMPS * RH, ATOMS),
        out_shape=jax.ShapeDtypeStruct((K, COMPS * RH, ATOMS), bf16),
        compiler_params=params(("arbitrary",)),
        cost_estimate=pl.CostEstimate(
            flops=2 * 4096 * 256 * WIDTH, bytes_accessed=9_000_000, transcendentals=600_000
        ),
        name="probe_weights",
    )(geo, pack)


HOLDERS = (2, 3, 4, 5, 5, 4)


def column_root(slab_ref):
    return slab_ref[lax.axis_index("gx") * lax.axis_size("gy") + lax.axis_index("gy")]


def collect_kernel(slab_ref, *refs):
    *block_refs, low_ref, high_ref, out_ref = refs
    code = lax.axis_index("gz") ^ column_root(slab_ref)

    @pl.when(code == 0)
    def _():
        out_ref[...] = low_ref[...]

    @pl.when(code == 1)
    def _():
        out_ref[...] = high_ref[...]

    for block, holder in enumerate(HOLDERS):
        at = FACE if block >= 4 else 0

        @pl.when(code == holder)
        def _(block=block, at=at):
            out_ref[at : at + FACE, :] = block_refs[SENT.index(block)][...]

    @pl.when((code == 2) | (code == 3))
    def _():
        out_ref[FACE:, :] = jnp.zeros((HALF - FACE, COMPS * RH), bf16)

    @pl.when(code > 5)
    def _():
        out_ref[...] = jnp.zeros_like(out_ref)


def collect(slab, blocks, low, high):
    return pl.pallas_call(
        collect_kernel,
        in_specs=[pl.BlockSpec(memory_space=pltpu.SMEM)] + in_vmem(BLOCKS + 2),
        out_specs=pl.BlockSpec(memory_space=pltpu.VMEM),
        out_shape=jax.ShapeDtypeStruct((HALF, COMPS * RH), bf16),
        compiler_params=params(),
        name="collect",
    )(slab, *[blocks[b] for b in SENT], low, high)


def readout_kernel(slab_ref, idx_ref, weight_ref, near_ref, far_ref, out_ref, keys_ref, acc_ref):
    step = pl.program_id(0)

    @pl.when(step == 0)
    def _():
        root = column_root(slab_ref)
        code = lax.axis_index("gz") ^ root

        def fetch(at, rows, holder, start):
            place = code ^ holder
            start = pl.multiple_of(place // 2 * HALF + start, FACE)

            @pl.when(place % 2 == 0)
            def _():
                keys_ref[pl.ds(at, rows), :] = near_ref[pl.ds(start, rows), :]

            @pl.when(place % 2 == 1)
            def _():
                keys_ref[pl.ds(at, rows), :] = far_ref[pl.ds(start, rows), :]

        fetch(0, HALF, 0, 0)
        fetch(HALF, HALF, 1, 0)
        for block, holder in enumerate(HOLDERS):
            odd = (parity(0), parity(1), root % 2)[block // 2]
            face = jnp.where(odd == block % 2, block // 2 * 2 + 1, block // 2 * 2)
            at = pl.multiple_of(ATOMS + face * FACE, FACE)
            fetch(at, FACE, holder, FACE if block >= 4 else 0)
        acc_ref[...] = jnp.zeros_like(acc_ref)

    weight = jnp.concatenate([weight_ref[s] for s in range(WIDE)], axis=1)
    product = dot(keys_ref[...], weight)
    rows = lax.broadcasted_iota(jnp.int32, (TABLE, ATOMS), 0)
    total = acc_ref[...]
    for s in range(WIDE):
        chosen = rows == idx_ref[pl.ds(step * WIDE + s, 1), :]
        part = jnp.where(chosen, product[:, s * ATOMS : (s + 1) * ATOMS], 0.0)
        total = total + jnp.sum(part.reshape(TABLE // 8, 8, ATOMS), axis=0)
    acc_ref[...] = total

    @pl.when(step == STEPS - 1)
    def _():
        out_ref[...] = jnp.sum(acc_ref[...], axis=0, keepdims=True)


def readout(slab, idx, weight, near, far):
    return pl.pallas_call(
        readout_kernel,
        grid=(STEPS,),
        in_specs=[
            pl.BlockSpec(memory_space=pltpu.SMEM),
            whole(K, ATOMS),
            slots(COMPS * RH, ATOMS),
            whole(4 * HALF, COMPS * RH),
            whole(4 * HALF, COMPS * RH),
        ],
        out_specs=whole(1, ATOMS),
        scratch_shapes=[pltpu.VMEM((TABLE, COMPS * RH), bf16), pltpu.VMEM((8, ATOMS), f32)],
        out_shape=jax.ShapeDtypeStruct((1, ATOMS), f32),
        compiler_params=params(("arbitrary",)),
        name="readout",
    )(slab, idx, weight, near, far)


def exchange(blocks):
    landed = [None] * BLOCKS
    for block in SENT:
        axis, turn = AXES[block // 2], block % 2
        count = lax.axis_size(axis)
        pairs = [(i, partner(i, count, turn)) for i in range(count)]
        landed[block] = lax.ppermute(blocks[block], axis, pairs)
    return landed


def along_column(block, code):
    return lax.ppermute(block, "gz", [(i, i ^ code) for i in range(lax.axis_size("gz"))])


def column_keys(slab, blocks, low, high, probe_weight):
    landed = [None] * BLOCKS
    inner = lax.axis_size("gz")
    for block in SENT:
        axis, turn, holder = AXES[block // 2], block % 2, HOLDERS[block]
        outer = lax.axis_size(axis)
        if axis == "gz":
            pairs = [(i, partner(i, inner, turn) ^ holder) for i in range(inner)]
            landed[block] = lax.ppermute(blocks[block], axis, pairs)
        else:
            pairs = [
                (i * inner + j, partner(i, outer, turn) * inner + (j ^ holder))
                for i in range(outer)
                for j in range(inner)
            ]
            landed[block] = lax.ppermute(blocks[block], (axis, "gz"), pairs)
    mine = collect(slab, landed, low, along_column(high, 1))
    moved = [along_column(mine, code) for code in (6, 4, 2)][::-1]
    *moved, probe_weight = lax.optimization_barrier((*moved, probe_weight))
    near = jnp.concatenate([mine] + moved, axis=0)
    return near, along_column(near, 1), probe_weight


def local(
    features,
    species,
    octant_lists,
    neighbour_index,
    neighbour_count,
    edge_vectors,
    radial_in,
    species_emb,
    radial_mid,
    radial_out,
    mix_weight,
    gate_weight,
    probe_in,
    probe_mid,
    probe_proj,
    probe_vectors,
    probe_index,
    probe_count,
    slab_index,
):
    sel, *blocks = pick(octant_lists, features)
    ghosts = exchange(blocks)
    species_row = species.reshape(1, ATOMS)
    turned, geo, probe_geo, index, hidden, pack = prepare(
        (
            edge_vectors,
            neighbour_count.reshape(1, ATOMS),
            features,
            neighbour_index,
            probe_vectors,
            probe_count.reshape(1, ATOMS),
            species_row,
            radial_in,
            jnp.swapaxes(species_emb, 1, 2),
            radial_mid,
            radial_out,
            mix_weight,
            gate_weight,
            jnp.swapaxes(probe_proj, 1, 2),
            probe_in,
            probe_mid,
        )
    )
    for t in range(LAYERS):
        if t > 0:
            hidden = hidden_units(t, species_row, geo, pack)
        outs = layer(t, index, geo, hidden, turned, sel, ghosts, pack)
        if t < LAYERS - 1:
            turned = outs[0]
            ghosts = exchange(outs[1:])
    near, far, probe_weight = column_keys(
        slab_index, outs[1:7], outs[7], outs[8], probe_weights(probe_geo, pack)
    )
    density = readout(slab_index, probe_index, probe_weight, near, far)
    return (outs[0], density.reshape(ATOMS))


def solution(mesh):
    in_specs = (
        P(("gx", "gy", "gz"), None),
        P(("gx", "gy", "gz")),
        P(None, None, None, ("gx", "gy", "gz")),
        P(None, ("gx", "gy", "gz")),
        P(("gx", "gy", "gz")),
        P(None, None, ("gx", "gy", "gz")),
        P(),
        P(),
        P(),
        P(),
        P(),
        P(),
        P(),
        P(),
        P(),
        P(None, None, ("gx", "gy", "gz")),
        P(None, ("gx", "gy", "gz")),
        P(("gx", "gy", "gz")),
        P(),
    )
    out_specs = (P(("gx", "gy", "gz"), None), P(("gx", "gy", "gz")))
    return jax.shard_map(local, mesh=mesh, in_specs=in_specs, out_specs=out_specs, check_vma=False)
```

```python
import functools
import math

import jax
import jax.numpy as jnp
import numpy as np
from jax import lax
from jax.experimental import pallas as pl
from jax.experimental.pallas import tpu as pltpu
from jax.sharding import PartitionSpec as P

C = 96
COMPS = 16
WIDTH = C * COMPS
RH = 64
NB = 8
SPECIES = 89
K = 32
LAYERS = 3
ATOMS = 128
FACE = 32
GHOSTS = 192
TABLE = 320
PADDED = 384
HALF = 64
CUTOFF = 4.0
DEGREE = (0, 1, 1, 1, 2, 2, 2, 2, 2, 3, 3, 3, 3, 3, 3, 3)
STARTS = (0, 1, 4, 9)
WIDTHS = (1, 3, 5, 7)
STEP = 2
PAIRS = K // (2 * STEP)
PARTS = 3
WIDE = 16
STEPS = K // WIDE
ENV_ROW = 16
INDEX_ROW = 17
BASIS_ROW = 24
GEO_ROWS = 32

VMEM_LIMIT = 24 * 1024 * 1024
VMEM_MOST = 62 * 1024 * 1024

f32 = jnp.float32
bf16 = jnp.bfloat16
f8 = jnp.float8_e4m3fn


def dot(a, b):
    return lax.dot_general(a, b, (((1,), (0,)), ((), ())), preferred_element_type=f32)


def dot_tn(a, b):
    return lax.dot_general(a, b, (((0,), (0,)), ((), ())), preferred_element_type=f32)


def dot_nt(a, b):
    return lax.dot_general(a, b, (((1,), (1,)), ((), ())), preferred_element_type=f32)


def sigmoid(u):
    return 0.5 * jnp.tanh(0.5 * u) + 0.5


def silu(u):
    half = 0.5 * u
    return half * jnp.tanh(half) + half


def power_scale(largest):
    scale = jnp.ones_like(largest)
    inverse = jnp.ones_like(largest)
    for j in (64, 32, 16, 8, 4, 2, 1):
        up = largest * inverse > 224.0 * 2.0**j
        scale = jnp.where(up, scale * 2.0**j, scale)
        inverse = jnp.where(up, inverse * 2.0**-j, inverse)
    for j in (32, 16, 8, 4, 2, 1):
        down = largest * inverse * 2.0**j <= 448.0
        scale = jnp.where(down, scale * 2.0**-j, scale)
        inverse = jnp.where(down, inverse * 2.0**j, inverse)
    return scale, inverse


def harmonics(vx, vy, vz):
    x = vx * 0.5
    y = vy * 0.5
    z = vz * 0.5
    q = x * x + y * y + z * z
    zz = 5.0 * z * z - q
    return [
        jnp.ones_like(x),
        math.sqrt(3.0) * x,
        math.sqrt(3.0) * y,
        math.sqrt(3.0) * z,
        math.sqrt(15.0) * x * y,
        math.sqrt(15.0) * y * z,
        math.sqrt(5.0) / 2.0 * (3.0 * z * z - q),
        math.sqrt(15.0) * x * z,
        math.sqrt(15.0) / 2.0 * (x * x - y * y),
        math.sqrt(35.0 / 8.0) * y * (3.0 * x * x - y * y),
        math.sqrt(105.0) * x * y * z,
        math.sqrt(21.0 / 8.0) * y * zz,
        math.sqrt(7.0) / 2.0 * z * (5.0 * z * z - 3.0 * q),
        math.sqrt(21.0 / 8.0) * x * zz,
        math.sqrt(105.0) / 2.0 * z * (x * x - y * y),
        math.sqrt(35.0 / 8.0) * x * (x * x - 3.0 * y * y),
    ]


def params(semantics=None, limit=VMEM_LIMIT):
    return pltpu.CompilerParams(vmem_limit_bytes=limit, dimension_semantics=semantics)


def whole(*shape):
    return pl.BlockSpec(shape, lambda i: (0,) * len(shape))


def slots(*shape):
    return pl.BlockSpec((WIDE,) + shape, lambda i: (i,) + (0,) * len(shape))


def in_vmem(count):
    return [pl.BlockSpec(memory_space=pltpu.VMEM)] * count


def in_hbm(count):
    return [pl.BlockSpec(memory_space=pltpu.HBM)] * count


def like(array):
    return jax.ShapeDtypeStruct(array.shape, array.dtype)


AXES = ("gx", "gy", "gz")
BLOCKS = 6
SENT = (3, 5, 2, 0, 1, 4)


def partner(index, count, turn):
    return (index + 1) % count if index % 2 == turn else (index - 1) % count


def parity(axis_number):
    return lax.axis_index(AXES[axis_number]) % 2


def pick_kernel(lists_hbm, rows_hbm, sel_ref, *refs):
    out_refs = refs[:BLOCKS]
    lists_ref, rows_ref, sems = refs[BLOCKS:]
    rows_copy = pltpu.make_async_copy(rows_hbm, rows_ref, sems.at[0])
    rows_copy.start()
    lists_copy = pltpu.make_async_copy(lists_hbm, lists_ref, sems.at[1])
    lists_copy.start()
    lists_copy.wait()
    lists = jnp.concatenate(
        [lists_ref[i, j, k : k + 1, :] for i in (0, 1) for j in (0, 1) for k in (0, 1)], axis=0
    )
    entry = lax.broadcasted_iota(jnp.int32, (8, GHOSTS), 0)
    lane = lax.broadcasted_iota(jnp.int32, (8, GHOSTS), 1)
    spread = dot(lists.astype(f32).astype(bf16), (entry == lane % 8).astype(f32).astype(bf16))
    block, quarter = lane // FACE, (lane // 8) % 4
    odd = jnp.where(block < 2, parity(0), jnp.where(block < 4, parity(1), parity(2)))
    side = jnp.where(block % 2 == odd, 1, 0)
    high, low = quarter // 2, quarter % 2
    octant = jnp.where(
        block < 2, 4 * side + quarter, jnp.where(block < 4, 4 * high + 2 * side + low, 2 * quarter + side)
    )
    chosen = jnp.sum(jnp.where(entry == octant, spread, 0.0), axis=0, keepdims=True)
    atom = lax.broadcasted_iota(jnp.int32, (ATOMS, GHOSTS), 0)
    turned_sel = (atom == chosen.astype(jnp.int32)).astype(f32)
    sel = turned_sel.T.astype(bf16)
    sel_ref[...] = sel
    rows_copy.wait()
    picked = dot(sel, rows_ref[...]).astype(bf16)
    for number, out_ref in enumerate(out_refs):
        out_ref[...] = picked[number * FACE : (number + 1) * FACE]


def pick(lists, rows):
    return pl.pallas_call(
        pick_kernel,
        grid=(1,),
        in_specs=in_hbm(2),
        out_specs=[whole(GHOSTS, ATOMS)] + [whole(FACE, WIDTH)] * BLOCKS,
        out_shape=[jax.ShapeDtypeStruct((GHOSTS, ATOMS), bf16)]
        + [jax.ShapeDtypeStruct((FACE, WIDTH), bf16)] * BLOCKS,
        scratch_shapes=[
            pltpu.VMEM(lists.shape, jnp.int32),
            pltpu.VMEM(rows.shape, bf16),
            pltpu.SemaphoreType.DMA((2,)),
        ],
        compiler_params=params(limit=VMEM_MOST),
        name="pick",
    )(lists, rows)


def geometry_into(vec_ref, count_ref, geo_ref, index_ref=None):
    sharpness = ((NB - 1) / CUTOFF) ** 2
    centers = lax.broadcasted_iota(jnp.int32, (NB, ATOMS), 0).astype(f32) * (CUTOFF / (NB - 1))

    def one_slot(k, carry):
        vx = vec_ref[0, pl.ds(k, 1), :]
        vy = vec_ref[1, pl.ds(k, 1), :]
        vz = vec_ref[2, pl.ds(k, 1), :]
        square = vx * vx + vy * vy + vz * vz
        shape = 1.0 - square / (CUTOFF * CUTOFF)
        valid = (k < count_ref[...]).astype(f32)
        envelope = shape * shape * valid * (K ** (-0.5))
        radius = jnp.sqrt(square)
        offset = radius - centers
        for m, value in enumerate(harmonics(vx, vy, vz)):
            geo_ref[k, m : m + 1, :] = value
        geo_ref[k, ENV_ROW:BASIS_ROW, :] = jnp.broadcast_to(envelope, (8, ATOMS))
        if index_ref is not None:
            geo_ref[k, INDEX_ROW : INDEX_ROW + 1, :] = index_ref[pl.ds(k, 1), :]
        geo_ref[k, BASIS_ROW:GEO_ROWS, :] = jnp.exp(-sharpness * offset * offset)
        return carry

    lax.fori_loop(0, K, one_slot, 0, unroll=4)


OUT, MIX, GATE, MID, EMB, IN, LAYER_ROWS = 0, 192, 576, 672, 736, 800, 816
FIRST_HIDDEN = WIDTH
FIRST_LAYER = FIRST_HIDDEN + K * RH
FIRST_SEL = FIRST_LAYER + LAYER_ROWS
FIRST_ROWS = FIRST_SEL + GHOSTS
LATER_PROJ = (LAYERS - 1) * LAYER_ROWS
LATER_PROBE_IN = LATER_PROJ + 4 * RH
LATER_PROBE_MID = LATER_PROBE_IN + 16
LATER_SEL = LATER_PROBE_MID + RH
LATER_ROWS = LATER_SEL + GHOSTS
WEIGHTS = 9


def weights_at(t):
    return FIRST_LAYER if t == 0 else (t - 1) * LAYER_ROWS


def pack_weights(refs, first_ref, later_ref):
    win_ref, wemb_ref, wmid_ref, wout_ref, mix_ref, gate_ref, proj_ref, pin_ref, pmid_ref = refs

    def put(pack_ref, at, value):
        pack_ref[at : at + value.shape[0], : value.shape[1]] = value

    def padded(value):
        return jnp.concatenate([value, jnp.zeros_like(value)], axis=0)

    for t in range(LAYERS):
        pack_ref, base = first_ref if t == 0 else later_ref, weights_at(t)
        for j in range(3):
            put(pack_ref, base + OUT + RH * j, wout_ref[t, :, 128 * j : 128 * (j + 1)])
        for degree in range(4):
            put(pack_ref, base + MIX + C * degree, mix_ref[t, degree])
        put(pack_ref, base + GATE, gate_ref[t])
        put(pack_ref, base + MID, wmid_ref[t])
        put(pack_ref, base + EMB, wemb_ref[t])
        put(pack_ref, base + IN, padded(win_ref[t]))
    for degree in range(4):
        put(later_ref, LATER_PROJ + RH * degree, proj_ref[degree])
    put(later_ref, LATER_PROBE_IN, padded(pin_ref[...]))
    put(later_ref, LATER_PROBE_MID, pmid_ref[...])


def hidden_into(t, species_ref, geo_ref, pack_ref, put):
    base = weights_at(t)
    wemb = pack_ref[base + EMB : base + EMB + RH, :SPECIES]
    win = pack_ref[base + IN : base + IN + 16, :RH][:NB]
    wmid = pack_ref[base + MID : base + MID + RH, :RH]
    ids = lax.broadcasted_iota(jnp.int32, (SPECIES, ATOMS), 0)
    emb = dot(wemb, (ids == species_ref[...]).astype(f32).astype(bf16))
    for k in range(0, K, 8):
        basis = jnp.concatenate([geo_ref[k + s, BASIS_ROW:GEO_ROWS, :] for s in range(8)], axis=1)
        hidden = dot_tn(win, basis.astype(bf16)) + jnp.concatenate([emb] * 8, axis=1)
        hidden = silu(hidden).astype(bf16)
        hidden = silu(dot_tn(wmid, hidden)).astype(bf16)
        for s in range(8):
            put(k + s, hidden[:, s * ATOMS : (s + 1) * ATOMS])


INPUTS = 6 + WEIGHTS


def prepare_kernel(*refs):
    geo_ref, first_ref, later_ref = refs[INPUTS : INPUTS + 3]
    *landed, index_ref, sems = refs[INPUTS + 3 :]
    copies = [
        pltpu.make_async_copy(source, target, sems.at[number])
        for number, (source, target) in enumerate(zip(refs[:INPUTS], landed))
    ]
    for copy in copies:
        copy.start()
    old_ref, vec_ref, count_ref, rows_ref, species_ref, sel_ref = landed[:6]
    copies[0].wait()
    index = old_ref[...]
    block = (index - ATOMS) // FACE
    odd = jnp.where(block < 2, parity(0), jnp.where(block < 4, parity(1), parity(2)))
    moved = jnp.where(block % 2 == 0, index + FACE, index - FACE)
    index_ref[...] = jnp.where((index >= ATOMS) & (odd == 0), moved, index).astype(f32)
    copies[1].wait()
    copies[2].wait()
    geometry_into(vec_ref, count_ref, geo_ref, index_ref)
    copies[3].wait()
    first_ref[:WIDTH, :] = rows_ref[...].astype(f32).T.astype(bf16)
    for copy in copies[4:]:
        copy.wait()
    first_ref[FIRST_SEL:, :] = sel_ref[...]
    later_ref[LATER_SEL:, :] = sel_ref[...]
    pack_weights(landed[6:], first_ref, later_ref)

    def put(k, hidden):
        at = FIRST_HIDDEN + k * RH
        first_ref[at : at + RH, :] = hidden

    hidden_into(0, species_ref, geo_ref, first_ref, put)


def prepare(inputs):
    outs = [
        jax.ShapeDtypeStruct((K, GEO_ROWS, ATOMS), f32),
        jax.ShapeDtypeStruct((FIRST_ROWS, 128), bf16),
        jax.ShapeDtypeStruct((LATER_ROWS, 128), bf16),
    ]
    return pl.pallas_call(
        prepare_kernel,
        grid=(1,),
        in_specs=in_hbm(INPUTS),
        out_specs=[whole(*out.shape) for out in outs],
        out_shape=outs,
        scratch_shapes=[pltpu.VMEM(array.shape, array.dtype) for array in inputs]
        + [pltpu.VMEM((K, ATOMS), f32), pltpu.SemaphoreType.DMA((INPUTS,))],
        compiler_params=params(limit=VMEM_MOST),
        cost_estimate=pl.CostEstimate(flops=10_000_000, bytes_accessed=9_000_000, transcendentals=100_000),
        name="prepare",
    )(*inputs)


def hidden_kernel(t, species_ref, geo_ref, pack_ref, out_ref):
    def put(k, hidden):
        out_ref[k] = hidden

    hidden_into(t, species_ref, geo_ref, pack_ref, put)


def hidden_units(t, species, geo, later):
    return pl.pallas_call(
        functools.partial(hidden_kernel, t),
        grid=(1,),
        in_specs=[whole(1, ATOMS), whole(K, GEO_ROWS, ATOMS), whole(LATER_ROWS, 128)],
        out_specs=whole(K, RH, ATOMS),
        out_shape=jax.ShapeDtypeStruct((K, RH, ATOMS), bf16),
        compiler_params=params(),
        cost_estimate=pl.CostEstimate(
            flops=2 * 4096 * 256 * RH * 2, bytes_accessed=2_000_000, transcendentals=600_000
        ),
        name="hidden_units",
    )(species, geo, later)


def layer_kernel(t, *refs):
    last = t == LAYERS - 1
    base = weights_at(t)
    geo_ref, pack_ref, *refs = refs
    ghost_refs, refs = refs[:BLOCKS], refs[BLOCKS:]
    if t == 0:
        turned_ref = pack_ref
        sel = pack_ref[FIRST_SEL:FIRST_ROWS, :]

        def hidden_of(k):
            return pack_ref[pl.ds(pl.multiple_of(FIRST_HIDDEN + k * RH, RH), RH), :]

    else:
        turned_ref, hidden_ref, *refs = refs
        sel = pack_ref[LATER_SEL:LATER_ROWS, :]

        def hidden_of(k):
            return hidden_ref[k]

    out_refs = refs[:-5]
    table_ref, acc_ref, even_ref, odd_ref, rad_ref = refs[-5:]
    wout = jnp.concatenate(
        [pack_ref[base + OUT + RH * j : base + OUT + RH * (j + 1), :] for j in range(3)], axis=1
    )
    own = turned_ref[:WIDTH, :].astype(f32)
    ghosts = jnp.concatenate([ghost_refs[SENT.index(b)][...] for b in range(BLOCKS)], axis=0)
    ghosts = ghosts.astype(f32).T
    scale, inverse = power_scale(
        jnp.maximum(
            jnp.max(jnp.abs(own), axis=(0, 1), keepdims=True),
            jnp.max(jnp.abs(ghosts), axis=(0, 1), keepdims=True),
        )
    )
    for at, part in ((0, own), (ATOMS, ghosts)):
        lanes = part.shape[1]
        part = part * inverse
        high = part.astype(f8)
        table_ref[:, at : at + lanes] = high
        low = part - high.astype(f32)
        table_ref[:, PADDED + at : PADDED + at + lanes] = low.astype(f8)
    for at in (TABLE, PADDED + TABLE):
        table_ref[:, at : at + PADDED - TABLE] = jnp.zeros((WIDTH, PADDED - TABLE), f8)

    def front(first, slot):
        hidden = jnp.concatenate([hidden_of(first + s) for s in range(STEP)], axis=1)
        envelope = jnp.concatenate(
            [geo_ref[first + s, ENV_ROW : ENV_ROW + 1, :] for s in range(STEP)], axis=1
        )
        rad_ref[slot] = dot_tn(wout, hidden) * (envelope * scale)
        ids = lax.broadcasted_iota(jnp.int32, (PADDED, ATOMS), 0).astype(f32)
        hot = jnp.concatenate(
            [
                (ids == geo_ref[first + s, INDEX_ROW : INDEX_ROW + 1, :]).astype(f32)
                for s in range(STEP)
            ],
            axis=1,
        )
        hot = hot.astype(f8)
        return jnp.concatenate([hot, hot], axis=0)

    def back(first, got_ref, slot, keep, tiles):
        for tile in tiles:
            scalar = []
            weight = []
            for s in range(STEP):
                lanes = slice(s * ATOMS, (s + 1) * ATOMS)
                scalar.append(got_ref[tile : tile + 8, lanes])
                weight.append(
                    [rad_ref[slot, l * C + tile : l * C + tile + 8, lanes] for l in range(4)]
                )
            for m in range(COMPS):
                at = m * C + tile
                total = acc_ref[at : at + 8, :]
                for s in range(STEP):
                    if m == 0:
                        value = scalar[s]
                    else:
                        value = got_ref[at : at + 8, s * ATOMS : (s + 1) * ATOMS]
                        value = value + geo_ref[first + s, m : m + 1, :] * scalar[s]
                    total = total + weight[s][DEGREE[m]] * value
                acc_ref[at : at + 8, :] = total if keep is None else jnp.where(keep, total, 0.0)

    def one_step(first, slot, behind, keep):
        got_ref, behind_ref = (even_ref, odd_ref) if slot == 0 else (odd_ref, even_ref)
        hot = front(first, slot)
        for part in range(PARTS):
            back(behind, behind_ref, 1 - slot, keep, range(part * C // PARTS, (part + 1) * C // PARTS, 8))
            rows = slice(part * WIDTH // PARTS, (part + 1) * WIDTH // PARTS)
            got_ref[rows, :] = dot(table_ref[rows, :], hot)

    def two_steps(i, carry):
        first = i * (2 * STEP)
        one_step(first, 0, jnp.maximum(first - STEP, 0), i > 0)
        one_step(first + STEP, 1, first, None)
        return carry

    lax.fori_loop(0, PAIRS, two_steps, 0)
    back(K - STEP, odd_ref, 1, None, range(0, C, 8))

    message = [acc_ref[m * C : (m + 1) * C, :].astype(bf16) for m in range(COMPS)]
    gate = sigmoid(dot_tn(pack_ref[base + GATE : base + GATE + C, :C], message[0]))
    updated = []
    for degree in range(4):
        start, width = STARTS[degree], WIDTHS[degree]
        at = base + MIX + C * degree
        mixed = dot_tn(pack_ref[at : at + C, :C], jnp.concatenate(message[start : start + width], axis=1))
        for j in range(width):
            m = start + j
            part = mixed[:, j * ATOMS : (j + 1) * ATOMS]
            before = turned_ref[m * C : (m + 1) * C, :].astype(f32)
            change = silu(part) if degree == 0 else gate * part
            updated.append((before + change).astype(bf16))
    new = jnp.concatenate(updated, axis=0)
    if not last:
        out_refs[0][...] = new
        picked = dot_nt(sel, new).astype(bf16)
        for face in range(6):
            out_refs[1 + face][...] = picked[face * FACE : (face + 1) * FACE]
    else:
        ones = (
            lax.broadcasted_iota(jnp.int32, (ATOMS, ATOMS), 0)
            == lax.broadcasted_iota(jnp.int32, (ATOMS, ATOMS), 1)
        ).astype(f32).astype(bf16)
        out_refs[0][...] = dot_nt(ones, new).astype(bf16)
        keys = jnp.concatenate(
            [
                dot(pack_ref[LATER_PROJ + RH * l : LATER_PROJ + RH * (l + 1), :C], updated[m])
                for m, l in enumerate(DEGREE)
            ],
            axis=0,
        ).astype(bf16)
        rows = dot_nt(jnp.concatenate([sel, ones], axis=0), keys).astype(bf16)
        for face in range(6):
            out_refs[1 + face][...] = rows[face * FACE : (face + 1) * FACE]
        out_refs[7][...] = rows[GHOSTS : GHOSTS + HALF]
        out_refs[8][...] = rows[GHOSTS + HALF :]


def layer(t, geo, pack, ghosts, more):
    last = t == LAYERS - 1
    if last:
        shapes = [(ATOMS, WIDTH)] + [(FACE, COMPS * RH)] * 6 + [(HALF, COMPS * RH)] * 2
    else:
        shapes = [(WIDTH, ATOMS)] + [(FACE, WIDTH)] * 6
    lanes = STEP * ATOMS
    return pl.pallas_call(
        functools.partial(layer_kernel, t),
        grid=(1,),
        in_specs=[whole(K, GEO_ROWS, ATOMS), whole(*pack.shape)]
        + [whole(FACE, WIDTH)] * BLOCKS
        + [whole(*array.shape) for array in more],
        out_specs=[whole(*shape) for shape in shapes],
        out_shape=[jax.ShapeDtypeStruct(shape, bf16) for shape in shapes],
        scratch_shapes=[
            pltpu.VMEM((WIDTH, 2 * PADDED), f8),
            pltpu.VMEM((WIDTH, ATOMS), f32),
            pltpu.VMEM((WIDTH, lanes), f32),
            pltpu.VMEM((WIDTH, lanes), f32),
            pltpu.VMEM((2, 4 * C, lanes), f32),
        ],
        compiler_params=params(limit=VMEM_LIMIT),
        cost_estimate=pl.CostEstimate(
            flops=2 * 4096 * 512 * WIDTH, bytes_accessed=3_000_000, transcendentals=600_000
        ),
        name="layer",
    )(geo, pack, *[ghosts[b] for b in SENT], *more)


def probe_weights_kernel(vec_ref, count_ref, pack_ref, out_ref, geo_ref):
    step = pl.program_id(0)

    @pl.when(step == 0)
    def _():
        geometry_into(vec_ref, count_ref, geo_ref)

    win = pack_ref[LATER_PROBE_IN : LATER_PROBE_IN + 16, :RH][:NB]
    wmid = pack_ref[LATER_PROBE_MID : LATER_PROBE_MID + RH, :RH]
    first = step * WIDE
    basis = jnp.concatenate(
        [geo_ref[first + s, BASIS_ROW:GEO_ROWS, :] for s in range(WIDE)], axis=1
    )
    hidden = silu(dot_tn(win, basis.astype(bf16))).astype(bf16)
    hidden = silu(dot_tn(wmid, hidden)).astype(bf16).astype(f32)
    for s in range(WIDE):
        scaled = hidden[:, s * ATOMS : (s + 1) * ATOMS]
        scaled = scaled * geo_ref[first + s, ENV_ROW : ENV_ROW + 1, :]
        for m in range(COMPS):
            value = scaled if m == 0 else scaled * geo_ref[first + s, m : m + 1, :]
            out_ref[s, m * RH : (m + 1) * RH, :] = value.astype(bf16)


def probe_weights(vectors, count, pack):
    return pl.pallas_call(
        probe_weights_kernel,
        grid=(STEPS,),
        in_specs=[whole(3, K, ATOMS), whole(1, ATOMS), whole(LATER_ROWS, 128)],
        out_specs=slots(COMPS * RH, ATOMS),
        out_shape=jax.ShapeDtypeStruct((K, COMPS * RH, ATOMS), bf16),
        scratch_shapes=[pltpu.VMEM((K, GEO_ROWS, ATOMS), f32)],
        compiler_params=params(("arbitrary",)),
        cost_estimate=pl.CostEstimate(
            flops=2 * 4096 * 256 * WIDTH, bytes_accessed=9_000_000, transcendentals=600_000
        ),
        name="probe_weights",
    )(vectors, count, pack)


HOLDERS = (2, 3, 4, 5, 5, 4)


def column_root(slab_ref):
    return slab_ref[lax.axis_index("gx") * lax.axis_size("gy") + lax.axis_index("gy")]


def collect_kernel(slab_ref, *refs):
    *block_refs, low_ref, high_ref, out_ref = refs
    code = lax.axis_index("gz") ^ column_root(slab_ref)

    @pl.when(code == 0)
    def _():
        out_ref[...] = low_ref[...]

    @pl.when(code == 1)
    def _():
        out_ref[...] = high_ref[...]

    for block, holder in enumerate(HOLDERS):
        at = FACE if block >= 4 else 0

        @pl.when(code == holder)
        def _(block=block, at=at):
            out_ref[at : at + FACE, :] = block_refs[SENT.index(block)][...]

    @pl.when((code == 2) | (code == 3))
    def _():
        out_ref[FACE:, :] = jnp.zeros((HALF - FACE, COMPS * RH), bf16)

    @pl.when(code > 5)
    def _():
        out_ref[...] = jnp.zeros_like(out_ref)


def collect(slab, blocks, low, high):
    return pl.pallas_call(
        collect_kernel,
        in_specs=[pl.BlockSpec(memory_space=pltpu.SMEM)] + in_vmem(BLOCKS + 2),
        out_specs=pl.BlockSpec(memory_space=pltpu.VMEM),
        out_shape=jax.ShapeDtypeStruct((HALF, COMPS * RH), bf16),
        compiler_params=params(),
        name="collect",
    )(slab, *[blocks[b] for b in SENT], low, high)


def readout_kernel(slab_ref, idx_ref, weight_ref, near_ref, far_ref, out_ref, keys_ref, acc_ref):
    step = pl.program_id(0)

    @pl.when(step == 0)
    def _():
        root = column_root(slab_ref)
        code = lax.axis_index("gz") ^ root

        def fetch(at, rows, holder, start):
            place = code ^ holder
            start = pl.multiple_of(place // 2 * HALF + start, FACE)

            @pl.when(place % 2 == 0)
            def _():
                keys_ref[pl.ds(at, rows), :] = near_ref[pl.ds(start, rows), :]

            @pl.when(place % 2 == 1)
            def _():
                keys_ref[pl.ds(at, rows), :] = far_ref[pl.ds(start, rows), :]

        fetch(0, HALF, 0, 0)
        fetch(HALF, HALF, 1, 0)
        for block, holder in enumerate(HOLDERS):
            odd = (parity(0), parity(1), root % 2)[block // 2]
            face = jnp.where(odd == block % 2, block // 2 * 2 + 1, block // 2 * 2)
            at = pl.multiple_of(ATOMS + face * FACE, FACE)
            fetch(at, FACE, holder, FACE if block >= 4 else 0)
        acc_ref[...] = jnp.zeros_like(acc_ref)

    weight = jnp.concatenate([weight_ref[s] for s in range(WIDE)], axis=1)
    product = dot(keys_ref[...], weight)
    rows = lax.broadcasted_iota(jnp.int32, (TABLE, ATOMS), 0)
    total = acc_ref[...]
    for s in range(WIDE):
        chosen = rows == idx_ref[pl.ds(step * WIDE + s, 1), :]
        part = jnp.where(chosen, product[:, s * ATOMS : (s + 1) * ATOMS], 0.0)
        total = total + jnp.sum(part.reshape(TABLE // 8, 8, ATOMS), axis=0)
    acc_ref[...] = total

    @pl.when(step == STEPS - 1)
    def _():
        out_ref[...] = jnp.sum(acc_ref[...], axis=0, keepdims=True)


def readout(slab, idx, weight, near, far):
    return pl.pallas_call(
        readout_kernel,
        grid=(STEPS,),
        in_specs=[
            pl.BlockSpec(memory_space=pltpu.SMEM),
            whole(K, ATOMS),
            slots(COMPS * RH, ATOMS),
            whole(4 * HALF, COMPS * RH),
            whole(4 * HALF, COMPS * RH),
        ],
        out_specs=whole(1, ATOMS),
        scratch_shapes=[pltpu.VMEM((TABLE, COMPS * RH), bf16), pltpu.VMEM((8, ATOMS), f32)],
        out_shape=jax.ShapeDtypeStruct((1, ATOMS), f32),
        compiler_params=params(("arbitrary",)),
        name="readout",
    )(slab, idx, weight, near, far)


def exchange(blocks):
    landed = [None] * BLOCKS
    for block in SENT:
        axis, turn = AXES[block // 2], block % 2
        count = lax.axis_size(axis)
        pairs = [(i, partner(i, count, turn)) for i in range(count)]
        landed[block] = lax.ppermute(blocks[block], axis, pairs)
    return landed


def along_column(block, code):
    return lax.ppermute(block, "gz", [(i, i ^ code) for i in range(lax.axis_size("gz"))])


def column_keys(slab, blocks, low, high, probe_weight):
    landed = [None] * BLOCKS
    inner = lax.axis_size("gz")
    for block in SENT:
        axis, turn, holder = AXES[block // 2], block % 2, HOLDERS[block]
        outer = lax.axis_size(axis)
        if axis == "gz":
            pairs = [(i, partner(i, inner, turn) ^ holder) for i in range(inner)]
            landed[block] = lax.ppermute(blocks[block], axis, pairs)
        else:
            pairs = [
                (i * inner + j, partner(i, outer, turn) * inner + (j ^ holder))
                for i in range(outer)
                for j in range(inner)
            ]
            landed[block] = lax.ppermute(blocks[block], (axis, "gz"), pairs)
    mine = collect(slab, landed, low, along_column(high, 1))
    moved = [along_column(mine, code) for code in (6, 4, 2)][::-1]
    *moved, probe_weight = lax.optimization_barrier((*moved, probe_weight))
    near = jnp.concatenate([mine] + moved, axis=0)
    return near, along_column(near, 1), probe_weight


def local(
    features,
    species,
    octant_lists,
    neighbour_index,
    neighbour_count,
    edge_vectors,
    radial_in,
    species_emb,
    radial_mid,
    radial_out,
    mix_weight,
    gate_weight,
    probe_in,
    probe_mid,
    probe_proj,
    probe_vectors,
    probe_index,
    probe_count,
    slab_index,
):
    sel, *blocks = pick(octant_lists, features)
    ghosts = exchange(blocks)
    species_row = species.reshape(1, ATOMS)
    geo, first, later = prepare(
        (
            neighbour_index,
            edge_vectors,
            neighbour_count.reshape(1, ATOMS),
            features,
            species_row,
            sel,
            radial_in,
            jnp.swapaxes(species_emb, 1, 2),
            radial_mid,
            radial_out,
            mix_weight,
            gate_weight,
            jnp.swapaxes(probe_proj, 1, 2),
            probe_in,
            probe_mid,
        )
    )
    for t in range(LAYERS):
        if t == 0:
            outs = layer(t, geo, first, ghosts, ())
        else:
            outs = layer(t, geo, later, ghosts, (turned, hidden_units(t, species_row, geo, later)))
        if t < LAYERS - 1:
            turned = outs[0]
            ghosts = exchange(outs[1:])
    near, far, probe_weight = column_keys(
        slab_index,
        outs[1:7],
        outs[7],
        outs[8],
        probe_weights(probe_vectors, probe_count.reshape(1, ATOMS), later),
    )
    density = readout(slab_index, probe_index, probe_weight, near, far)
    return (outs[0], density.reshape(ATOMS))


def solution(mesh):
    in_specs = (
        P(("gx", "gy", "gz"), None),
        P(("gx", "gy", "gz")),
        P(None, None, None, ("gx", "gy", "gz")),
        P(None, ("gx", "gy", "gz")),
        P(("gx", "gy", "gz")),
        P(None, None, ("gx", "gy", "gz")),
        P(),
        P(),
        P(),
        P(),
        P(),
        P(),
        P(),
        P(),
        P(),
        P(None, None, ("gx", "gy", "gz")),
        P(None, ("gx", "gy", "gz")),
        P(("gx", "gy", "gz")),
        P(),
    )
    out_specs = (P(("gx", "gy", "gz"), None), P(("gx", "gy", "gz")))
    return jax.shard_map(local, mesh=mesh, in_specs=in_specs, out_specs=out_specs, check_vma=False)
```

```python
import functools
import math

import jax
import jax.numpy as jnp
import numpy as np
from jax import lax
from jax.experimental import pallas as pl
from jax.experimental.pallas import tpu as pltpu
from jax.sharding import PartitionSpec as P

C = 96
COMPS = 16
WIDTH = C * COMPS
RH = 64
NB = 8
SPECIES = 89
K = 32
LAYERS = 3
ATOMS = 128
FACE = 32
GHOSTS = 192
TABLE = 320
PADDED = 384
PART = 48
REST = 16
CUTOFF = 4.0
DEGREE = (0, 1, 1, 1, 2, 2, 2, 2, 2, 3, 3, 3, 3, 3, 3, 3)
STARTS = (0, 1, 4, 9)
WIDTHS = (1, 3, 5, 7)
STEP = 2
PAIRS = K // (2 * STEP)
PARTS = 3
WIDE = 16
STEPS = K // WIDE
ENV_ROW = 16
INDEX_ROW = 17
BASIS_ROW = 24
GEO_ROWS = 32

VMEM_LIMIT = 24 * 1024 * 1024
VMEM_MOST = 62 * 1024 * 1024

f32 = jnp.float32
bf16 = jnp.bfloat16
f8 = jnp.float8_e4m3fn


def dot(a, b):
    return lax.dot_general(a, b, (((1,), (0,)), ((), ())), preferred_element_type=f32)


def dot_tn(a, b):
    return lax.dot_general(a, b, (((0,), (0,)), ((), ())), preferred_element_type=f32)


def dot_nt(a, b):
    return lax.dot_general(a, b, (((1,), (1,)), ((), ())), preferred_element_type=f32)


def sigmoid(u):
    return 0.5 * jnp.tanh(0.5 * u) + 0.5


def silu(u):
    half = 0.5 * u
    return half * jnp.tanh(half) + half


def power_scale(largest):
    scale = jnp.ones_like(largest)
    inverse = jnp.ones_like(largest)
    for j in (64, 32, 16, 8, 4, 2, 1):
        up = largest * inverse > 224.0 * 2.0**j
        scale = jnp.where(up, scale * 2.0**j, scale)
        inverse = jnp.where(up, inverse * 2.0**-j, inverse)
    for j in (32, 16, 8, 4, 2, 1):
        down = largest * inverse * 2.0**j <= 448.0
        scale = jnp.where(down, scale * 2.0**-j, scale)
        inverse = jnp.where(down, inverse * 2.0**j, inverse)
    return scale, inverse


def harmonics(vx, vy, vz):
    x = vx * 0.5
    y = vy * 0.5
    z = vz * 0.5
    q = x * x + y * y + z * z
    zz = 5.0 * z * z - q
    return [
        jnp.ones_like(x),
        math.sqrt(3.0) * x,
        math.sqrt(3.0) * y,
        math.sqrt(3.0) * z,
        math.sqrt(15.0) * x * y,
        math.sqrt(15.0) * y * z,
        math.sqrt(5.0) / 2.0 * (3.0 * z * z - q),
        math.sqrt(15.0) * x * z,
        math.sqrt(15.0) / 2.0 * (x * x - y * y),
        math.sqrt(35.0 / 8.0) * y * (3.0 * x * x - y * y),
        math.sqrt(105.0) * x * y * z,
        math.sqrt(21.0 / 8.0) * y * zz,
        math.sqrt(7.0) / 2.0 * z * (5.0 * z * z - 3.0 * q),
        math.sqrt(21.0 / 8.0) * x * zz,
        math.sqrt(105.0) / 2.0 * z * (x * x - y * y),
        math.sqrt(35.0 / 8.0) * x * (x * x - 3.0 * y * y),
    ]


def params(semantics=None, limit=VMEM_LIMIT):
    return pltpu.CompilerParams(vmem_limit_bytes=limit, dimension_semantics=semantics)


def whole(*shape):
    return pl.BlockSpec(shape, lambda i: (0,) * len(shape))


def slots(*shape):
    return pl.BlockSpec((WIDE,) + shape, lambda i: (i,) + (0,) * len(shape))


def in_vmem(count):
    return [pl.BlockSpec(memory_space=pltpu.VMEM)] * count


def in_hbm(count):
    return [pl.BlockSpec(memory_space=pltpu.HBM)] * count


def like(array):
    return jax.ShapeDtypeStruct(array.shape, array.dtype)


AXES = ("gx", "gy", "gz")
BLOCKS = 6
SENT = (3, 5, 2, 0, 1, 4)


def partner(index, count, turn):
    return (index + 1) % count if index % 2 == turn else (index - 1) % count


def parity(axis_number):
    return lax.axis_index(AXES[axis_number]) % 2


def pick_kernel(lists_hbm, rows_hbm, sel_ref, *refs):
    out_refs = refs[:BLOCKS]
    lists_ref, rows_ref, sems = refs[BLOCKS:]
    rows_copy = pltpu.make_async_copy(rows_hbm, rows_ref, sems.at[0])
    rows_copy.start()
    lists_copy = pltpu.make_async_copy(lists_hbm, lists_ref, sems.at[1])
    lists_copy.start()
    lists_copy.wait()
    lists = jnp.concatenate(
        [lists_ref[i, j, k : k + 1, :] for i in (0, 1) for j in (0, 1) for k in (0, 1)], axis=0
    )
    entry = lax.broadcasted_iota(jnp.int32, (8, GHOSTS), 0)
    lane = lax.broadcasted_iota(jnp.int32, (8, GHOSTS), 1)
    spread = dot(lists.astype(f32).astype(bf16), (entry == lane % 8).astype(f32).astype(bf16))
    block, quarter = lane // FACE, (lane // 8) % 4
    odd = jnp.where(block < 2, parity(0), jnp.where(block < 4, parity(1), parity(2)))
    side = jnp.where(block % 2 == odd, 1, 0)
    high, low = quarter // 2, quarter % 2
    octant = jnp.where(
        block < 2, 4 * side + quarter, jnp.where(block < 4, 4 * high + 2 * side + low, 2 * quarter + side)
    )
    chosen = jnp.sum(jnp.where(entry == octant, spread, 0.0), axis=0, keepdims=True)
    atom = lax.broadcasted_iota(jnp.int32, (ATOMS, GHOSTS), 0)
    turned_sel = (atom == chosen.astype(jnp.int32)).astype(f32)
    sel = turned_sel.T.astype(bf16)
    sel_ref[...] = sel
    rows_copy.wait()
    picked = dot(sel, rows_ref[...]).astype(bf16)
    for number, out_ref in enumerate(out_refs):
        out_ref[...] = picked[number * FACE : (number + 1) * FACE]


def pick(lists, rows):
    return pl.pallas_call(
        pick_kernel,
        grid=(1,),
        in_specs=in_hbm(2),
        out_specs=[whole(GHOSTS, ATOMS)] + [whole(FACE, WIDTH)] * BLOCKS,
        out_shape=[jax.ShapeDtypeStruct((GHOSTS, ATOMS), bf16)]
        + [jax.ShapeDtypeStruct((FACE, WIDTH), bf16)] * BLOCKS,
        scratch_shapes=[
            pltpu.VMEM(lists.shape, jnp.int32),
            pltpu.VMEM(rows.shape, bf16),
            pltpu.SemaphoreType.DMA((2,)),
        ],
        compiler_params=params(limit=VMEM_MOST),
        name="pick",
    )(lists, rows)


def geometry_into(vec_ref, count_ref, geo_ref, index_ref=None):
    sharpness = ((NB - 1) / CUTOFF) ** 2
    centers = lax.broadcasted_iota(jnp.int32, (NB, ATOMS), 0).astype(f32) * (CUTOFF / (NB - 1))

    def one_slot(k, carry):
        vx = vec_ref[0, pl.ds(k, 1), :]
        vy = vec_ref[1, pl.ds(k, 1), :]
        vz = vec_ref[2, pl.ds(k, 1), :]
        square = vx * vx + vy * vy + vz * vz
        shape = 1.0 - square / (CUTOFF * CUTOFF)
        valid = (k < count_ref[...]).astype(f32)
        envelope = shape * shape * valid * (K ** (-0.5))
        radius = jnp.sqrt(square)
        offset = radius - centers
        for m, value in enumerate(harmonics(vx, vy, vz)):
            geo_ref[k, m : m + 1, :] = value
        geo_ref[k, ENV_ROW:BASIS_ROW, :] = jnp.broadcast_to(envelope, (8, ATOMS))
        if index_ref is not None:
            geo_ref[k, INDEX_ROW : INDEX_ROW + 1, :] = index_ref[pl.ds(k, 1), :]
        geo_ref[k, BASIS_ROW:GEO_ROWS, :] = jnp.exp(-sharpness * offset * offset)
        return carry

    lax.fori_loop(0, K, one_slot, 0, unroll=4)


OUT, MIX, GATE, MID, EMB, IN, LAYER_ROWS = 0, 192, 576, 672, 736, 800, 816
FIRST_HIDDEN = WIDTH
FIRST_LAYER = FIRST_HIDDEN + K * RH
FIRST_SEL = FIRST_LAYER + LAYER_ROWS
FIRST_ROWS = FIRST_SEL + GHOSTS
LATER_PROJ = (LAYERS - 1) * LAYER_ROWS
LATER_PROBE_IN = LATER_PROJ + 4 * RH
LATER_PROBE_MID = LATER_PROBE_IN + 16
LATER_SEL = LATER_PROBE_MID + RH
LATER_ROWS = LATER_SEL + GHOSTS
WEIGHTS = 9


def weights_at(t):
    return FIRST_LAYER if t == 0 else (t - 1) * LAYER_ROWS


def pack_weights(refs, first_ref, later_ref):
    win_ref, wemb_ref, wmid_ref, wout_ref, mix_ref, gate_ref, proj_ref, pin_ref, pmid_ref = refs

    def put(pack_ref, at, value):
        pack_ref[at : at + value.shape[0], : value.shape[1]] = value

    def padded(value):
        return jnp.concatenate([value, jnp.zeros_like(value)], axis=0)

    for t in range(LAYERS):
        pack_ref, base = first_ref if t == 0 else later_ref, weights_at(t)
        for j in range(3):
            put(pack_ref, base + OUT + RH * j, wout_ref[t, :, 128 * j : 128 * (j + 1)])
        for degree in range(4):
            put(pack_ref, base + MIX + C * degree, mix_ref[t, degree])
        put(pack_ref, base + GATE, gate_ref[t])
        put(pack_ref, base + MID, wmid_ref[t])
        put(pack_ref, base + EMB, wemb_ref[t])
        put(pack_ref, base + IN, padded(win_ref[t]))
    for degree in range(4):
        put(later_ref, LATER_PROJ + RH * degree, proj_ref[degree])
    put(later_ref, LATER_PROBE_IN, padded(pin_ref[...]))
    put(later_ref, LATER_PROBE_MID, pmid_ref[...])


def hidden_into(t, species_ref, geo_ref, pack_ref, put):
    base = weights_at(t)
    wemb = pack_ref[base + EMB : base + EMB + RH, :SPECIES]
    win = pack_ref[base + IN : base + IN + 16, :RH][:NB]
    wmid = pack_ref[base + MID : base + MID + RH, :RH]
    ids = lax.broadcasted_iota(jnp.int32, (SPECIES, ATOMS), 0)
    emb = dot(wemb, (ids == species_ref[...]).astype(f32).astype(bf16))
    for k in range(0, K, 8):
        basis = jnp.concatenate([geo_ref[k + s, BASIS_ROW:GEO_ROWS, :] for s in range(8)], axis=1)
        hidden = dot_tn(win, basis.astype(bf16)) + jnp.concatenate([emb] * 8, axis=1)
        hidden = silu(hidden).astype(bf16)
        hidden = silu(dot_tn(wmid, hidden)).astype(bf16)
        for s in range(8):
            put(k + s, hidden[:, s * ATOMS : (s + 1) * ATOMS])


INPUTS = 6 + WEIGHTS


def prepare_kernel(*refs):
    geo_ref, first_ref, later_ref = refs[INPUTS : INPUTS + 3]
    *landed, index_ref, sems = refs[INPUTS + 3 :]
    copies = [
        pltpu.make_async_copy(source, target, sems.at[number])
        for number, (source, target) in enumerate(zip(refs[:INPUTS], landed))
    ]
    for copy in copies:
        copy.start()
    old_ref, vec_ref, count_ref, rows_ref, species_ref, sel_ref = landed[:6]
    copies[0].wait()
    index = old_ref[...]
    block = (index - ATOMS) // FACE
    odd = jnp.where(block < 2, parity(0), jnp.where(block < 4, parity(1), parity(2)))
    moved = jnp.where(block % 2 == 0, index + FACE, index - FACE)
    index_ref[...] = jnp.where((index >= ATOMS) & (odd == 0), moved, index).astype(f32)
    copies[1].wait()
    copies[2].wait()
    geometry_into(vec_ref, count_ref, geo_ref, index_ref)
    copies[3].wait()
    first_ref[:WIDTH, :] = rows_ref[...].astype(f32).T.astype(bf16)
    for copy in copies[4:]:
        copy.wait()
    first_ref[FIRST_SEL:, :] = sel_ref[...]
    later_ref[LATER_SEL:, :] = sel_ref[...]
    pack_weights(landed[6:], first_ref, later_ref)

    def put(k, hidden):
        at = FIRST_HIDDEN + k * RH
        first_ref[at : at + RH, :] = hidden

    hidden_into(0, species_ref, geo_ref, first_ref, put)


def prepare(inputs):
    outs = [
        jax.ShapeDtypeStruct((K, GEO_ROWS, ATOMS), f32),
        jax.ShapeDtypeStruct((FIRST_ROWS, 128), bf16),
        jax.ShapeDtypeStruct((LATER_ROWS, 128), bf16),
    ]
    return pl.pallas_call(
        prepare_kernel,
        grid=(1,),
        in_specs=in_hbm(INPUTS),
        out_specs=[whole(*out.shape) for out in outs],
        out_shape=outs,
        scratch_shapes=[pltpu.VMEM(array.shape, array.dtype) for array in inputs]
        + [pltpu.VMEM((K, ATOMS), f32), pltpu.SemaphoreType.DMA((INPUTS,))],
        compiler_params=params(limit=VMEM_MOST),
        cost_estimate=pl.CostEstimate(flops=10_000_000, bytes_accessed=9_000_000, transcendentals=100_000),
        name="prepare",
    )(*inputs)


def hidden_kernel(t, species_ref, geo_ref, pack_ref, out_ref):
    def put(k, hidden):
        out_ref[k] = hidden

    hidden_into(t, species_ref, geo_ref, pack_ref, put)


def hidden_units(t, species, geo, later):
    return pl.pallas_call(
        functools.partial(hidden_kernel, t),
        grid=(1,),
        in_specs=[whole(1, ATOMS), whole(K, GEO_ROWS, ATOMS), whole(LATER_ROWS, 128)],
        out_specs=whole(K, RH, ATOMS),
        out_shape=jax.ShapeDtypeStruct((K, RH, ATOMS), bf16),
        compiler_params=params(),
        cost_estimate=pl.CostEstimate(
            flops=2 * 4096 * 256 * RH * 2, bytes_accessed=2_000_000, transcendentals=600_000
        ),
        name="hidden_units",
    )(species, geo, later)


def layer_kernel(t, *refs):
    last = t == LAYERS - 1
    base = weights_at(t)
    geo_ref, pack_ref, *refs = refs
    ghost_refs, refs = refs[:BLOCKS], refs[BLOCKS:]
    if t == 0:
        turned_ref = pack_ref
        sel = pack_ref[FIRST_SEL:FIRST_ROWS, :]

        def hidden_of(k):
            return pack_ref[pl.ds(pl.multiple_of(FIRST_HIDDEN + k * RH, RH), RH), :]

    else:
        turned_ref, hidden_ref, *refs = refs
        sel = pack_ref[LATER_SEL:LATER_ROWS, :]

        def hidden_of(k):
            return hidden_ref[k]

    out_refs = refs[:-5]
    table_ref, acc_ref, even_ref, odd_ref, rad_ref = refs[-5:]
    wout = jnp.concatenate(
        [pack_ref[base + OUT + RH * j : base + OUT + RH * (j + 1), :] for j in range(3)], axis=1
    )
    own = turned_ref[:WIDTH, :].astype(f32)
    ghosts = jnp.concatenate([ghost_refs[SENT.index(b)][...] for b in range(BLOCKS)], axis=0)
    ghosts = ghosts.astype(f32).T
    scale, inverse = power_scale(
        jnp.maximum(
            jnp.max(jnp.abs(own), axis=(0, 1), keepdims=True),
            jnp.max(jnp.abs(ghosts), axis=(0, 1), keepdims=True),
        )
    )
    for at, part in ((0, own), (ATOMS, ghosts)):
        lanes = part.shape[1]
        part = part * inverse
        high = part.astype(f8)
        table_ref[:, at : at + lanes] = high
        low = part - high.astype(f32)
        table_ref[:, PADDED + at : PADDED + at + lanes] = low.astype(f8)
    for at in (TABLE, PADDED + TABLE):
        table_ref[:, at : at + PADDED - TABLE] = jnp.zeros((WIDTH, PADDED - TABLE), f8)

    def front(first, slot):
        hidden = jnp.concatenate([hidden_of(first + s) for s in range(STEP)], axis=1)
        envelope = jnp.concatenate(
            [geo_ref[first + s, ENV_ROW : ENV_ROW + 1, :] for s in range(STEP)], axis=1
        )
        rad_ref[slot] = dot_tn(wout, hidden) * (envelope * scale)
        ids = lax.broadcasted_iota(jnp.int32, (PADDED, ATOMS), 0).astype(f32)
        hot = jnp.concatenate(
            [
                (ids == geo_ref[first + s, INDEX_ROW : INDEX_ROW + 1, :]).astype(f32)
                for s in range(STEP)
            ],
            axis=1,
        )
        hot = hot.astype(f8)
        return jnp.concatenate([hot, hot], axis=0)

    def back(first, got_ref, slot, keep, tiles):
        for tile in tiles:
            scalar = []
            weight = []
            for s in range(STEP):
                lanes = slice(s * ATOMS, (s + 1) * ATOMS)
                scalar.append(got_ref[tile : tile + 8, lanes])
                weight.append(
                    [rad_ref[slot, l * C + tile : l * C + tile + 8, lanes] for l in range(4)]
                )
            for m in range(COMPS):
                at = m * C + tile
                total = acc_ref[at : at + 8, :]
                for s in range(STEP):
                    if m == 0:
                        value = scalar[s]
                    else:
                        value = got_ref[at : at + 8, s * ATOMS : (s + 1) * ATOMS]
                        value = value + geo_ref[first + s, m : m + 1, :] * scalar[s]
                    total = total + weight[s][DEGREE[m]] * value
                acc_ref[at : at + 8, :] = total if keep is None else jnp.where(keep, total, 0.0)

    def one_step(first, slot, behind, keep):
        got_ref, behind_ref = (even_ref, odd_ref) if slot == 0 else (odd_ref, even_ref)
        hot = front(first, slot)
        for part in range(PARTS):
            back(behind, behind_ref, 1 - slot, keep, range(part * C // PARTS, (part + 1) * C // PARTS, 8))
            rows = slice(part * WIDTH // PARTS, (part + 1) * WIDTH // PARTS)
            got_ref[rows, :] = dot(table_ref[rows, :], hot)

    def two_steps(i, carry):
        first = i * (2 * STEP)
        one_step(first, 0, jnp.maximum(first - STEP, 0), i > 0)
        one_step(first + STEP, 1, first, None)
        return carry

    lax.fori_loop(0, PAIRS, two_steps, 0)
    back(K - STEP, odd_ref, 1, None, range(0, C, 8))

    message = [acc_ref[m * C : (m + 1) * C, :].astype(bf16) for m in range(COMPS)]
    gate = sigmoid(dot_tn(pack_ref[base + GATE : base + GATE + C, :C], message[0]))
    updated = []
    for degree in range(4):
        start, width = STARTS[degree], WIDTHS[degree]
        at = base + MIX + C * degree
        mixed = dot_tn(pack_ref[at : at + C, :C], jnp.concatenate(message[start : start + width], axis=1))
        for j in range(width):
            m = start + j
            part = mixed[:, j * ATOMS : (j + 1) * ATOMS]
            before = turned_ref[m * C : (m + 1) * C, :].astype(f32)
            change = silu(part) if degree == 0 else gate * part
            updated.append((before + change).astype(bf16))
    new = jnp.concatenate(updated, axis=0)
    if not last:
        out_refs[0][...] = new
        picked = dot_nt(sel, new).astype(bf16)
        for face in range(6):
            out_refs[1 + face][...] = picked[face * FACE : (face + 1) * FACE]
    else:
        ones = (
            lax.broadcasted_iota(jnp.int32, (ATOMS, ATOMS), 0)
            == lax.broadcasted_iota(jnp.int32, (ATOMS, ATOMS), 1)
        ).astype(f32).astype(bf16)
        out_refs[0][...] = dot_nt(ones, new).astype(bf16)
        keys = jnp.concatenate(
            [
                dot(pack_ref[LATER_PROJ + RH * l : LATER_PROJ + RH * (l + 1), :C], updated[m])
                for m, l in enumerate(DEGREE)
            ],
            axis=0,
        ).astype(bf16)
        rows = dot_nt(jnp.concatenate([sel, ones], axis=0), keys).astype(bf16)
        for face in range(6):
            out_refs[1 + face][:FACE, :] = rows[face * FACE : (face + 1) * FACE]
        own = rows[GHOSTS:]
        out_refs[5][FACE:, :] = own[2 * PART : 2 * PART + REST]
        out_refs[7][...] = own[:PART]
        out_refs[8][...] = own[PART : 2 * PART]
        out_refs[9][...] = own[2 * PART + REST :]


def layer(t, geo, pack, ghosts, more):
    last = t == LAYERS - 1
    if last:
        counts = (FACE, FACE, FACE, FACE, PART, FACE, PART, PART, REST)
        shapes = [(ATOMS, WIDTH)] + [(count, COMPS * RH) for count in counts]
    else:
        shapes = [(WIDTH, ATOMS)] + [(FACE, WIDTH)] * 6
    lanes = STEP * ATOMS
    return pl.pallas_call(
        functools.partial(layer_kernel, t),
        grid=(1,),
        in_specs=[whole(K, GEO_ROWS, ATOMS), whole(*pack.shape)]
        + [whole(FACE, WIDTH)] * BLOCKS
        + [whole(*array.shape) for array in more],
        out_specs=[whole(*shape) for shape in shapes],
        out_shape=[jax.ShapeDtypeStruct(shape, bf16) for shape in shapes],
        scratch_shapes=[
            pltpu.VMEM((WIDTH, 2 * PADDED), f8),
            pltpu.VMEM((WIDTH, ATOMS), f32),
            pltpu.VMEM((WIDTH, lanes), f32),
            pltpu.VMEM((WIDTH, lanes), f32),
            pltpu.VMEM((2, 4 * C, lanes), f32),
        ],
        compiler_params=params(limit=VMEM_LIMIT),
        cost_estimate=pl.CostEstimate(
            flops=2 * 4096 * 512 * WIDTH, bytes_accessed=3_000_000, transcendentals=600_000
        ),
        name="layer",
    )(geo, pack, *[ghosts[b] for b in SENT], *more)


def probe_weights_kernel(vec_ref, count_ref, pack_ref, out_ref, geo_ref):
    step = pl.program_id(0)

    @pl.when(step == 0)
    def _():
        geometry_into(vec_ref, count_ref, geo_ref)

    win = pack_ref[LATER_PROBE_IN : LATER_PROBE_IN + 16, :RH][:NB]
    wmid = pack_ref[LATER_PROBE_MID : LATER_PROBE_MID + RH, :RH]
    first = step * WIDE
    basis = jnp.concatenate(
        [geo_ref[first + s, BASIS_ROW:GEO_ROWS, :] for s in range(WIDE)], axis=1
    )
    hidden = silu(dot_tn(win, basis.astype(bf16))).astype(bf16)
    hidden = silu(dot_tn(wmid, hidden)).astype(bf16).astype(f32)
    for s in range(WIDE):
        scaled = hidden[:, s * ATOMS : (s + 1) * ATOMS]
        scaled = scaled * geo_ref[first + s, ENV_ROW : ENV_ROW + 1, :]
        for m in range(COMPS):
            value = scaled if m == 0 else scaled * geo_ref[first + s, m : m + 1, :]
            out_ref[s, m * RH : (m + 1) * RH, :] = value.astype(bf16)


def probe_weights(vectors, count, pack):
    return pl.pallas_call(
        probe_weights_kernel,
        grid=(STEPS,),
        in_specs=[whole(3, K, ATOMS), whole(1, ATOMS), whole(LATER_ROWS, 128)],
        out_specs=slots(COMPS * RH, ATOMS),
        out_shape=jax.ShapeDtypeStruct((K, COMPS * RH, ATOMS), bf16),
        scratch_shapes=[pltpu.VMEM((K, GEO_ROWS, ATOMS), f32)],
        compiler_params=params(("arbitrary",)),
        cost_estimate=pl.CostEstimate(
            flops=2 * 4096 * 256 * WIDTH, bytes_accessed=9_000_000, transcendentals=600_000
        ),
        name="probe_weights",
    )(vectors, count, pack)


HOLDERS = (2, 3, 4, 5, 7, 6)


def column_root(slab_ref):
    return slab_ref[lax.axis_index("gx") * lax.axis_size("gy") + lax.axis_index("gy")]


def collect_kernel(slab_ref, *refs):
    *block_refs, low_ref, high_ref, rest_ref, out_ref = refs
    code = lax.axis_index("gz") ^ column_root(slab_ref)

    @pl.when(code == 0)
    def _():
        out_ref[...] = low_ref[...]

    @pl.when(code == 1)
    def _():
        out_ref[...] = high_ref[...]

    for block, holder in enumerate(HOLDERS):

        @pl.when(code == holder)
        def _(block=block, holder=holder):
            out_ref[:FACE, :] = block_refs[SENT.index(block)][:FACE, :]
            if holder == 6:
                out_ref[FACE:, :] = block_refs[SENT.index(4)][FACE:, :]
            elif holder == 2:
                out_ref[FACE:, :] = rest_ref[...]
            else:
                out_ref[FACE:, :] = jnp.zeros((REST, COMPS * RH), bf16)


def collect(slab, blocks, low, high, rest):
    return pl.pallas_call(
        collect_kernel,
        in_specs=[pl.BlockSpec(memory_space=pltpu.SMEM)] + in_vmem(BLOCKS + 3),
        out_specs=pl.BlockSpec(memory_space=pltpu.VMEM),
        out_shape=jax.ShapeDtypeStruct((PART, COMPS * RH), bf16),
        compiler_params=params(),
        name="collect",
    )(slab, *[blocks[b] for b in SENT], low, high, rest)


def readout_kernel(slab_ref, idx_ref, weight_ref, near_ref, far_ref, out_ref, keys_ref, acc_ref):
    step = pl.program_id(0)

    @pl.when(step == 0)
    def _():
        root = column_root(slab_ref)
        code = lax.axis_index("gz") ^ root

        def fetch(at, rows, holder, start):
            place = code ^ holder
            start = pl.multiple_of(place // 2 * PART + start, REST)

            @pl.when(place % 2 == 0)
            def _():
                keys_ref[pl.ds(at, rows), :] = near_ref[pl.ds(start, rows), :]

            @pl.when(place % 2 == 1)
            def _():
                keys_ref[pl.ds(at, rows), :] = far_ref[pl.ds(start, rows), :]

        fetch(0, PART, 0, 0)
        fetch(PART, PART, 1, 0)
        fetch(2 * PART, REST, 6, FACE)
        fetch(2 * PART + REST, REST, 2, FACE)
        for block, holder in enumerate(HOLDERS):
            odd = (parity(0), parity(1), root % 2)[block // 2]
            face = jnp.where(odd == block % 2, block // 2 * 2 + 1, block // 2 * 2)
            at = pl.multiple_of(ATOMS + face * FACE, FACE)
            fetch(at, FACE, holder, 0)
        acc_ref[...] = jnp.zeros_like(acc_ref)

    weight = jnp.concatenate([weight_ref[s] for s in range(WIDE)], axis=1)
    product = dot(keys_ref[...], weight)
    rows = lax.broadcasted_iota(jnp.int32, (TABLE, ATOMS), 0)
    total = acc_ref[...]
    for s in range(WIDE):
        chosen = rows == idx_ref[pl.ds(step * WIDE + s, 1), :]
        part = jnp.where(chosen, product[:, s * ATOMS : (s + 1) * ATOMS], 0.0)
        total = total + jnp.sum(part.reshape(TABLE // 8, 8, ATOMS), axis=0)
    acc_ref[...] = total

    @pl.when(step == STEPS - 1)
    def _():
        out_ref[...] = jnp.sum(acc_ref[...], axis=0, keepdims=True)


def readout(slab, idx, weight, near, far):
    return pl.pallas_call(
        readout_kernel,
        grid=(STEPS,),
        in_specs=[
            pl.BlockSpec(memory_space=pltpu.SMEM),
            whole(K, ATOMS),
            slots(COMPS * RH, ATOMS),
            whole(4 * PART, COMPS * RH),
            whole(4 * PART, COMPS * RH),
        ],
        out_specs=whole(1, ATOMS),
        scratch_shapes=[pltpu.VMEM((TABLE, COMPS * RH), bf16), pltpu.VMEM((8, ATOMS), f32)],
        out_shape=jax.ShapeDtypeStruct((1, ATOMS), f32),
        compiler_params=params(("arbitrary",)),
        name="readout",
    )(slab, idx, weight, near, far)


def exchange(blocks):
    landed = [None] * BLOCKS
    for block in SENT:
        axis, turn = AXES[block // 2], block % 2
        count = lax.axis_size(axis)
        pairs = [(i, partner(i, count, turn)) for i in range(count)]
        landed[block] = lax.ppermute(blocks[block], axis, pairs)
    return landed


def along_column(block, code):
    return lax.ppermute(block, "gz", [(i, i ^ code) for i in range(lax.axis_size("gz"))])


def column_keys(slab, blocks, low, high, rest, probe_weight):
    landed = [None] * BLOCKS
    inner = lax.axis_size("gz")
    for block in SENT:
        axis, turn, holder = AXES[block // 2], block % 2, HOLDERS[block]
        outer = lax.axis_size(axis)
        if axis == "gz":
            pairs = [(i, partner(i, inner, turn) ^ holder) for i in range(inner)]
            landed[block] = lax.ppermute(blocks[block], axis, pairs)
        else:
            pairs = [
                (i * inner + j, partner(i, outer, turn) * inner + (j ^ holder))
                for i in range(outer)
                for j in range(inner)
            ]
            landed[block] = lax.ppermute(blocks[block], (axis, "gz"), pairs)
    mine = collect(slab, landed, low, along_column(high, 1), along_column(rest, 2))
    moved = [along_column(mine, code) for code in (6, 4, 2)][::-1]
    *moved, probe_weight = lax.optimization_barrier((*moved, probe_weight))
    near = jnp.concatenate([mine] + moved, axis=0)
    return near, along_column(near, 1), probe_weight


def local(
    features,
    species,
    octant_lists,
    neighbour_index,
    neighbour_count,
    edge_vectors,
    radial_in,
    species_emb,
    radial_mid,
    radial_out,
    mix_weight,
    gate_weight,
    probe_in,
    probe_mid,
    probe_proj,
    probe_vectors,
    probe_index,
    probe_count,
    slab_index,
):
    sel, *blocks = pick(octant_lists, features)
    ghosts = exchange(blocks)
    species_row = species.reshape(1, ATOMS)
    geo, first, later = prepare(
        (
            neighbour_index,
            edge_vectors,
            neighbour_count.reshape(1, ATOMS),
            features,
            species_row,
            sel,
            radial_in,
            jnp.swapaxes(species_emb, 1, 2),
            radial_mid,
            radial_out,
            mix_weight,
            gate_weight,
            jnp.swapaxes(probe_proj, 1, 2),
            probe_in,
            probe_mid,
        )
    )
    for t in range(LAYERS):
        if t == 0:
            outs = layer(t, geo, first, ghosts, ())
        else:
            outs = layer(t, geo, later, ghosts, (turned, hidden_units(t, species_row, geo, later)))
        if t < LAYERS - 1:
            turned = outs[0]
            ghosts = exchange(outs[1:])
    near, far, probe_weight = column_keys(
        slab_index,
        outs[1:7],
        outs[7],
        outs[8],
        outs[9],
        probe_weights(probe_vectors, probe_count.reshape(1, ATOMS), later),
    )
    density = readout(slab_index, probe_index, probe_weight, near, far)
    return (outs[0], density.reshape(ATOMS))


def solution(mesh):
    in_specs = (
        P(("gx", "gy", "gz"), None),
        P(("gx", "gy", "gz")),
        P(None, None, None, ("gx", "gy", "gz")),
        P(None, ("gx", "gy", "gz")),
        P(("gx", "gy", "gz")),
        P(None, None, ("gx", "gy", "gz")),
        P(),
        P(),
        P(),
        P(),
        P(),
        P(),
        P(),
        P(),
        P(),
        P(None, None, ("gx", "gy", "gz")),
        P(None, ("gx", "gy", "gz")),
        P(("gx", "gy", "gz")),
        P(),
    )
    out_specs = (P(("gx", "gy", "gz"), None), P(("gx", "gy", "gz")))
    return jax.shard_map(local, mesh=mesh, in_specs=in_specs, out_specs=out_specs, check_vma=False)
```

```python
import functools
import math

import jax
import jax.numpy as jnp
import numpy as np
from jax import lax
from jax.experimental import pallas as pl
from jax.experimental.pallas import tpu as pltpu
from jax.sharding import PartitionSpec as P

C = 96
COMPS = 16
WIDTH = C * COMPS
RH = 64
NB = 8
SPECIES = 89
K = 32
LAYERS = 3
ATOMS = 128
FACE = 32
GHOSTS = 192
TABLE = 320
PADDED = 384
PART = 48
REST = 16
CUTOFF = 4.0
DEGREE = (0, 1, 1, 1, 2, 2, 2, 2, 2, 3, 3, 3, 3, 3, 3, 3)
STARTS = (0, 1, 4, 9)
WIDTHS = (1, 3, 5, 7)
STEP = 2
PAIRS = K // (2 * STEP)
PARTS = 3
WIDE = 8
STEPS = K // WIDE
ENV_ROW = 16
INDEX_ROW = 17
BASIS_ROW = 24
GEO_ROWS = 32

VMEM_LIMIT = 24 * 1024 * 1024
VMEM_MOST = 62 * 1024 * 1024

f32 = jnp.float32
bf16 = jnp.bfloat16
f8 = jnp.float8_e4m3fn


def dot(a, b):
    return lax.dot_general(a, b, (((1,), (0,)), ((), ())), preferred_element_type=f32)


def dot_tn(a, b):
    return lax.dot_general(a, b, (((0,), (0,)), ((), ())), preferred_element_type=f32)


def dot_nt(a, b):
    return lax.dot_general(a, b, (((1,), (1,)), ((), ())), preferred_element_type=f32)


def sigmoid(u):
    return 0.5 * jnp.tanh(0.5 * u) + 0.5


def silu(u):
    half = 0.5 * u
    return half * jnp.tanh(half) + half


def power_scale(largest):
    scale = jnp.ones_like(largest)
    inverse = jnp.ones_like(largest)
    for j in (64, 32, 16, 8, 4, 2, 1):
        up = largest * inverse > 224.0 * 2.0**j
        scale = jnp.where(up, scale * 2.0**j, scale)
        inverse = jnp.where(up, inverse * 2.0**-j, inverse)
    for j in (32, 16, 8, 4, 2, 1):
        down = largest * inverse * 2.0**j <= 448.0
        scale = jnp.where(down, scale * 2.0**-j, scale)
        inverse = jnp.where(down, inverse * 2.0**j, inverse)
    return scale, inverse


def harmonics(vx, vy, vz):
    x = vx * 0.5
    y = vy * 0.5
    z = vz * 0.5
    q = x * x + y * y + z * z
    zz = 5.0 * z * z - q
    return [
        jnp.ones_like(x),
        math.sqrt(3.0) * x,
        math.sqrt(3.0) * y,
        math.sqrt(3.0) * z,
        math.sqrt(15.0) * x * y,
        math.sqrt(15.0) * y * z,
        math.sqrt(5.0) / 2.0 * (3.0 * z * z - q),
        math.sqrt(15.0) * x * z,
        math.sqrt(15.0) / 2.0 * (x * x - y * y),
        math.sqrt(35.0 / 8.0) * y * (3.0 * x * x - y * y),
        math.sqrt(105.0) * x * y * z,
        math.sqrt(21.0 / 8.0) * y * zz,
        math.sqrt(7.0) / 2.0 * z * (5.0 * z * z - 3.0 * q),
        math.sqrt(21.0 / 8.0) * x * zz,
        math.sqrt(105.0) / 2.0 * z * (x * x - y * y),
        math.sqrt(35.0 / 8.0) * x * (x * x - 3.0 * y * y),
    ]


def params(semantics=None, limit=VMEM_LIMIT):
    return pltpu.CompilerParams(vmem_limit_bytes=limit, dimension_semantics=semantics)


def whole(*shape):
    return pl.BlockSpec(shape, lambda i: (0,) * len(shape))


def slots(*shape):
    return pl.BlockSpec((WIDE,) + shape, lambda i: (i,) + (0,) * len(shape))


def in_vmem(count):
    return [pl.BlockSpec(memory_space=pltpu.VMEM)] * count


def in_hbm(count):
    return [pl.BlockSpec(memory_space=pltpu.HBM)] * count


def like(array):
    return jax.ShapeDtypeStruct(array.shape, array.dtype)


AXES = ("gx", "gy", "gz")
BLOCKS = 6
SENT = (3, 5, 2, 0, 1, 4)


def partner(index, count, turn):
    return (index + 1) % count if index % 2 == turn else (index - 1) % count


def parity(axis_number):
    return lax.axis_index(AXES[axis_number]) % 2


def pick_kernel(lists_hbm, rows_hbm, sel_ref, *refs):
    out_refs = refs[:BLOCKS]
    lists_ref, rows_ref, sems = refs[BLOCKS:]
    rows_copy = pltpu.make_async_copy(rows_hbm, rows_ref, sems.at[0])
    rows_copy.start()
    lists_copy = pltpu.make_async_copy(lists_hbm, lists_ref, sems.at[1])
    lists_copy.start()
    lists_copy.wait()
    lists = jnp.concatenate(
        [lists_ref[i, j, k : k + 1, :] for i in (0, 1) for j in (0, 1) for k in (0, 1)], axis=0
    )
    entry = lax.broadcasted_iota(jnp.int32, (8, GHOSTS), 0)
    lane = lax.broadcasted_iota(jnp.int32, (8, GHOSTS), 1)
    spread = dot(lists.astype(f32).astype(bf16), (entry == lane % 8).astype(f32).astype(bf16))
    block, quarter = lane // FACE, (lane // 8) % 4
    odd = jnp.where(block < 2, parity(0), jnp.where(block < 4, parity(1), parity(2)))
    side = jnp.where(block % 2 == odd, 1, 0)
    high, low = quarter // 2, quarter % 2
    octant = jnp.where(
        block < 2, 4 * side + quarter, jnp.where(block < 4, 4 * high + 2 * side + low, 2 * quarter + side)
    )
    chosen = jnp.sum(jnp.where(entry == octant, spread, 0.0), axis=0, keepdims=True)
    atom = lax.broadcasted_iota(jnp.int32, (ATOMS, GHOSTS), 0)
    turned_sel = (atom == chosen.astype(jnp.int32)).astype(f32)
    sel = turned_sel.T.astype(bf16)
    sel_ref[...] = sel
    rows_copy.wait()
    picked = dot(sel, rows_ref[...]).astype(bf16)
    for number, out_ref in enumerate(out_refs):
        out_ref[...] = picked[number * FACE : (number + 1) * FACE]


def pick(lists, rows):
    return pl.pallas_call(
        pick_kernel,
        grid=(1,),
        in_specs=in_hbm(2),
        out_specs=[whole(GHOSTS, ATOMS)] + [whole(FACE, WIDTH)] * BLOCKS,
        out_shape=[jax.ShapeDtypeStruct((GHOSTS, ATOMS), bf16)]
        + [jax.ShapeDtypeStruct((FACE, WIDTH), bf16)] * BLOCKS,
        scratch_shapes=[
            pltpu.VMEM(lists.shape, jnp.int32),
            pltpu.VMEM(rows.shape, bf16),
            pltpu.SemaphoreType.DMA((2,)),
        ],
        compiler_params=params(limit=VMEM_MOST),
        name="pick",
    )(lists, rows)


def geometry_into(vec_ref, count_ref, geo_ref, index_ref=None):
    sharpness = ((NB - 1) / CUTOFF) ** 2
    centers = lax.broadcasted_iota(jnp.int32, (NB, ATOMS), 0).astype(f32) * (CUTOFF / (NB - 1))

    def one_slot(k, carry):
        vx = vec_ref[0, pl.ds(k, 1), :]
        vy = vec_ref[1, pl.ds(k, 1), :]
        vz = vec_ref[2, pl.ds(k, 1), :]
        square = vx * vx + vy * vy + vz * vz
        shape = 1.0 - square / (CUTOFF * CUTOFF)
        valid = (k < count_ref[...]).astype(f32)
        envelope = shape * shape * valid * (K ** (-0.5))
        radius = jnp.sqrt(square)
        offset = radius - centers
        for m, value in enumerate(harmonics(vx, vy, vz)):
            geo_ref[k, m : m + 1, :] = value
        geo_ref[k, ENV_ROW:BASIS_ROW, :] = jnp.broadcast_to(envelope, (8, ATOMS))
        if index_ref is not None:
            geo_ref[k, INDEX_ROW : INDEX_ROW + 1, :] = index_ref[pl.ds(k, 1), :]
        geo_ref[k, BASIS_ROW:GEO_ROWS, :] = jnp.exp(-sharpness * offset * offset)
        return carry

    lax.fori_loop(0, K, one_slot, 0, unroll=4)


OUT, MIX, GATE, MID, EMB, IN, LAYER_ROWS = 0, 192, 576, 672, 736, 800, 816
FIRST_HIDDEN = WIDTH
FIRST_LAYER = FIRST_HIDDEN + K * RH
FIRST_SEL = FIRST_LAYER + LAYER_ROWS
FIRST_ROWS = FIRST_SEL + GHOSTS
LATER_PROJ = (LAYERS - 1) * LAYER_ROWS
LATER_PROBE_IN = LATER_PROJ + 4 * RH
LATER_PROBE_MID = LATER_PROBE_IN + 16
LATER_SEL = LATER_PROBE_MID + RH
LATER_ROWS = LATER_SEL + GHOSTS
WEIGHTS = 9


def weights_at(t):
    return FIRST_LAYER if t == 0 else (t - 1) * LAYER_ROWS


def pack_weights(refs, first_ref, later_ref):
    win_ref, wemb_ref, wmid_ref, wout_ref, mix_ref, gate_ref, proj_ref, pin_ref, pmid_ref = refs

    def put(pack_ref, at, value):
        pack_ref[at : at + value.shape[0], : value.shape[1]] = value

    def padded(value):
        return jnp.concatenate([value, jnp.zeros_like(value)], axis=0)

    for t in range(LAYERS):
        pack_ref, base = first_ref if t == 0 else later_ref, weights_at(t)
        for j in range(3):
            put(pack_ref, base + OUT + RH * j, wout_ref[t, :, 128 * j : 128 * (j + 1)])
        for degree in range(4):
            put(pack_ref, base + MIX + C * degree, mix_ref[t, degree])
        put(pack_ref, base + GATE, gate_ref[t])
        put(pack_ref, base + MID, wmid_ref[t])
        put(pack_ref, base + EMB, wemb_ref[t])
        put(pack_ref, base + IN, padded(win_ref[t]))
    for degree in range(4):
        put(later_ref, LATER_PROJ + RH * degree, proj_ref[degree])
    put(later_ref, LATER_PROBE_IN, padded(pin_ref[...]))
    put(later_ref, LATER_PROBE_MID, pmid_ref[...])


def hidden_into(t, species_ref, geo_ref, pack_ref, put):
    base = weights_at(t)
    wemb = pack_ref[base + EMB : base + EMB + RH, :SPECIES]
    win = pack_ref[base + IN : base + IN + 16, :RH][:NB]
    wmid = pack_ref[base + MID : base + MID + RH, :RH]
    ids = lax.broadcasted_iota(jnp.int32, (SPECIES, ATOMS), 0)
    emb = dot(wemb, (ids == species_ref[...]).astype(f32).astype(bf16))
    for k in range(0, K, 8):
        basis = jnp.concatenate([geo_ref[k + s, BASIS_ROW:GEO_ROWS, :] for s in range(8)], axis=1)
        hidden = dot_tn(win, basis.astype(bf16)) + jnp.concatenate([emb] * 8, axis=1)
        hidden = silu(hidden).astype(bf16)
        hidden = silu(dot_tn(wmid, hidden)).astype(bf16)
        for s in range(8):
            put(k + s, hidden[:, s * ATOMS : (s + 1) * ATOMS])


INPUTS = 6 + WEIGHTS


def prepare_kernel(*refs):
    geo_ref, first_ref, later_ref = refs[INPUTS : INPUTS + 3]
    *landed, index_ref, sems = refs[INPUTS + 3 :]
    copies = [
        pltpu.make_async_copy(source, target, sems.at[number])
        for number, (source, target) in enumerate(zip(refs[:INPUTS], landed))
    ]
    for copy in copies:
        copy.start()
    old_ref, vec_ref, count_ref, rows_ref, species_ref, sel_ref = landed[:6]
    copies[0].wait()
    index = old_ref[...]
    block = (index - ATOMS) // FACE
    odd = jnp.where(block < 2, parity(0), jnp.where(block < 4, parity(1), parity(2)))
    moved = jnp.where(block % 2 == 0, index + FACE, index - FACE)
    index_ref[...] = jnp.where((index >= ATOMS) & (odd == 0), moved, index).astype(f32)
    copies[1].wait()
    copies[2].wait()
    geometry_into(vec_ref, count_ref, geo_ref, index_ref)
    copies[3].wait()
    first_ref[:WIDTH, :] = rows_ref[...].astype(f32).T.astype(bf16)
    for copy in copies[4:]:
        copy.wait()
    first_ref[FIRST_SEL:, :] = sel_ref[...]
    later_ref[LATER_SEL:, :] = sel_ref[...]
    pack_weights(landed[6:], first_ref, later_ref)

    def put(k, hidden):
        at = FIRST_HIDDEN + k * RH
        first_ref[at : at + RH, :] = hidden

    hidden_into(0, species_ref, geo_ref, first_ref, put)


def prepare(inputs):
    outs = [
        jax.ShapeDtypeStruct((K, GEO_ROWS, ATOMS), f32),
        jax.ShapeDtypeStruct((FIRST_ROWS, 128), bf16),
        jax.ShapeDtypeStruct((LATER_ROWS, 128), bf16),
    ]
    return pl.pallas_call(
        prepare_kernel,
        grid=(1,),
        in_specs=in_hbm(INPUTS),
        out_specs=[whole(*out.shape) for out in outs],
        out_shape=outs,
        scratch_shapes=[pltpu.VMEM(array.shape, array.dtype) for array in inputs]
        + [pltpu.VMEM((K, ATOMS), f32), pltpu.SemaphoreType.DMA((INPUTS,))],
        compiler_params=params(limit=VMEM_MOST),
        cost_estimate=pl.CostEstimate(flops=10_000_000, bytes_accessed=9_000_000, transcendentals=100_000),
        name="prepare",
    )(*inputs)


def hidden_kernel(t, species_ref, geo_ref, pack_ref, out_ref):
    def put(k, hidden):
        out_ref[k] = hidden

    hidden_into(t, species_ref, geo_ref, pack_ref, put)


def hidden_units(t, species, geo, later):
    return pl.pallas_call(
        functools.partial(hidden_kernel, t),
        grid=(1,),
        in_specs=[whole(1, ATOMS), whole(K, GEO_ROWS, ATOMS), whole(LATER_ROWS, 128)],
        out_specs=whole(K, RH, ATOMS),
        out_shape=jax.ShapeDtypeStruct((K, RH, ATOMS), bf16),
        compiler_params=params(),
        cost_estimate=pl.CostEstimate(
            flops=2 * 4096 * 256 * RH * 2, bytes_accessed=2_000_000, transcendentals=600_000
        ),
        name="hidden_units",
    )(species, geo, later)


def layer_kernel(t, *refs):
    last = t == LAYERS - 1
    base = weights_at(t)
    geo_ref, pack_ref, *refs = refs
    ghost_refs, refs = refs[:BLOCKS], refs[BLOCKS:]
    if t == 0:
        turned_ref = pack_ref
        sel = pack_ref[FIRST_SEL:FIRST_ROWS, :]

        def hidden_of(k):
            return pack_ref[pl.ds(pl.multiple_of(FIRST_HIDDEN + k * RH, RH), RH), :]

    else:
        turned_ref, hidden_ref, *refs = refs
        sel = pack_ref[LATER_SEL:LATER_ROWS, :]

        def hidden_of(k):
            return hidden_ref[k]

    out_refs = refs[:-5]
    table_ref, acc_ref, even_ref, odd_ref, rad_ref = refs[-5:]
    wout = jnp.concatenate(
        [pack_ref[base + OUT + RH * j : base + OUT + RH * (j + 1), :] for j in range(3)], axis=1
    )
    own = turned_ref[:WIDTH, :].astype(f32)
    ghosts = jnp.concatenate([ghost_refs[SENT.index(b)][...] for b in range(BLOCKS)], axis=0)
    ghosts = ghosts.astype(f32).T
    scale, inverse = power_scale(
        jnp.maximum(
            jnp.max(jnp.abs(own), axis=(0, 1), keepdims=True),
            jnp.max(jnp.abs(ghosts), axis=(0, 1), keepdims=True),
        )
    )
    for at, part in ((0, own), (ATOMS, ghosts)):
        lanes = part.shape[1]
        part = part * inverse
        high = part.astype(f8)
        table_ref[:, at : at + lanes] = high
        low = part - high.astype(f32)
        table_ref[:, PADDED + at : PADDED + at + lanes] = low.astype(f8)
    for at in (TABLE, PADDED + TABLE):
        table_ref[:, at : at + PADDED - TABLE] = jnp.zeros((WIDTH, PADDED - TABLE), f8)

    def front(first, slot):
        hidden = jnp.concatenate([hidden_of(first + s) for s in range(STEP)], axis=1)
        envelope = jnp.concatenate(
            [geo_ref[first + s, ENV_ROW : ENV_ROW + 1, :] for s in range(STEP)], axis=1
        )
        rad_ref[slot] = dot_tn(wout, hidden) * (envelope * scale)
        ids = lax.broadcasted_iota(jnp.int32, (PADDED, ATOMS), 0).astype(f32)
        hot = jnp.concatenate(
            [
                (ids == geo_ref[first + s, INDEX_ROW : INDEX_ROW + 1, :]).astype(f32)
                for s in range(STEP)
            ],
            axis=1,
        )
        hot = hot.astype(f8)
        return jnp.concatenate([hot, hot], axis=0)

    def back(first, got_ref, slot, keep, tiles):
        for tile in tiles:
            scalar = []
            weight = []
            for s in range(STEP):
                lanes = slice(s * ATOMS, (s + 1) * ATOMS)
                scalar.append(got_ref[tile : tile + 8, lanes])
                weight.append(
                    [rad_ref[slot, l * C + tile : l * C + tile + 8, lanes] for l in range(4)]
                )
            for m in range(COMPS):
                at = m * C + tile
                total = acc_ref[at : at + 8, :]
                for s in range(STEP):
                    if m == 0:
                        value = scalar[s]
                    else:
                        value = got_ref[at : at + 8, s * ATOMS : (s + 1) * ATOMS]
                        value = value + geo_ref[first + s, m : m + 1, :] * scalar[s]
                    total = total + weight[s][DEGREE[m]] * value
                acc_ref[at : at + 8, :] = total if keep is None else jnp.where(keep, total, 0.0)

    def one_step(first, slot, behind, keep):
        got_ref, behind_ref = (even_ref, odd_ref) if slot == 0 else (odd_ref, even_ref)
        hot = front(first, slot)
        for part in range(PARTS):
            back(behind, behind_ref, 1 - slot, keep, range(part * C // PARTS, (part + 1) * C // PARTS, 8))
            rows = slice(part * WIDTH // PARTS, (part + 1) * WIDTH // PARTS)
            got_ref[rows, :] = dot(table_ref[rows, :], hot)

    def two_steps(i, carry):
        first = i * (2 * STEP)
        one_step(first, 0, jnp.maximum(first - STEP, 0), i > 0)
        one_step(first + STEP, 1, first, None)
        return carry

    lax.fori_loop(0, PAIRS, two_steps, 0)
    back(K - STEP, odd_ref, 1, None, range(0, C, 8))

    message = [acc_ref[m * C : (m + 1) * C, :].astype(bf16) for m in range(COMPS)]
    gate = sigmoid(dot_tn(pack_ref[base + GATE : base + GATE + C, :C], message[0]))
    updated = []
    for degree in range(4):
        start, width = STARTS[degree], WIDTHS[degree]
        at = base + MIX + C * degree
        mixed = dot_tn(pack_ref[at : at + C, :C], jnp.concatenate(message[start : start + width], axis=1))
        for j in range(width):
            m = start + j
            part = mixed[:, j * ATOMS : (j + 1) * ATOMS]
            before = turned_ref[m * C : (m + 1) * C, :].astype(f32)
            change = silu(part) if degree == 0 else gate * part
            updated.append((before + change).astype(bf16))
    new = jnp.concatenate(updated, axis=0)
    if not last:
        out_refs[0][...] = new
        picked = dot_nt(sel, new).astype(bf16)
        for face in range(6):
            out_refs[1 + face][...] = picked[face * FACE : (face + 1) * FACE]
    else:
        ones = (
            lax.broadcasted_iota(jnp.int32, (ATOMS, ATOMS), 0)
            == lax.broadcasted_iota(jnp.int32, (ATOMS, ATOMS), 1)
        ).astype(f32).astype(bf16)
        out_refs[0][...] = dot_nt(ones, new).astype(bf16)
        keys = jnp.concatenate(
            [
                dot(pack_ref[LATER_PROJ + RH * l : LATER_PROJ + RH * (l + 1), :C], updated[m])
                for m, l in enumerate(DEGREE)
            ],
            axis=0,
        ).astype(bf16)
        rows = dot_nt(jnp.concatenate([sel, ones], axis=0), keys).astype(bf16)
        for face in range(6):
            out_refs[1 + face][:FACE, :] = rows[face * FACE : (face + 1) * FACE]
        own = rows[GHOSTS:]
        out_refs[5][FACE:, :] = own[2 * PART : 2 * PART + REST]
        out_refs[7][...] = own[:PART]
        out_refs[8][...] = own[PART : 2 * PART]
        out_refs[9][...] = own[2 * PART + REST :]


def layer(t, geo, pack, ghosts, more):
    last = t == LAYERS - 1
    if last:
        counts = (FACE, FACE, FACE, FACE, PART, FACE, PART, PART, REST)
        shapes = [(ATOMS, WIDTH)] + [(count, COMPS * RH) for count in counts]
    else:
        shapes = [(WIDTH, ATOMS)] + [(FACE, WIDTH)] * 6
    lanes = STEP * ATOMS
    return pl.pallas_call(
        functools.partial(layer_kernel, t),
        grid=(1,),
        in_specs=[whole(K, GEO_ROWS, ATOMS), whole(*pack.shape)]
        + [whole(FACE, WIDTH)] * BLOCKS
        + [whole(*array.shape) for array in more],
        out_specs=[whole(*shape) for shape in shapes],
        out_shape=[jax.ShapeDtypeStruct(shape, bf16) for shape in shapes],
        scratch_shapes=[
            pltpu.VMEM((WIDTH, 2 * PADDED), f8),
            pltpu.VMEM((WIDTH, ATOMS), f32),
            pltpu.VMEM((WIDTH, lanes), f32),
            pltpu.VMEM((WIDTH, lanes), f32),
            pltpu.VMEM((2, 4 * C, lanes), f32),
        ],
        compiler_params=params(limit=VMEM_LIMIT),
        cost_estimate=pl.CostEstimate(
            flops=2 * 4096 * 512 * WIDTH, bytes_accessed=3_000_000, transcendentals=600_000
        ),
        name="layer",
    )(geo, pack, *[ghosts[b] for b in SENT], *more)


def probe_weights_kernel(vec_ref, count_ref, pack_ref, out_ref, geo_ref):
    step = pl.program_id(0)

    @pl.when(step == 0)
    def _():
        geometry_into(vec_ref, count_ref, geo_ref)

    win = pack_ref[LATER_PROBE_IN : LATER_PROBE_IN + 16, :RH][:NB]
    wmid = pack_ref[LATER_PROBE_MID : LATER_PROBE_MID + RH, :RH]
    first = step * WIDE
    basis = jnp.concatenate(
        [geo_ref[first + s, BASIS_ROW:GEO_ROWS, :] for s in range(WIDE)], axis=1
    )
    hidden = silu(dot_tn(win, basis.astype(bf16))).astype(bf16)
    hidden = silu(dot_tn(wmid, hidden)).astype(bf16).astype(f32)
    for s in range(WIDE):
        scaled = hidden[:, s * ATOMS : (s + 1) * ATOMS]
        scaled = scaled * geo_ref[first + s, ENV_ROW : ENV_ROW + 1, :]
        for m in range(COMPS):
            value = scaled if m == 0 else scaled * geo_ref[first + s, m : m + 1, :]
            out_ref[s, m * RH : (m + 1) * RH, :] = value.astype(bf16)


def probe_weights(vectors, count, pack):
    return pl.pallas_call(
        probe_weights_kernel,
        grid=(STEPS,),
        in_specs=[whole(3, K, ATOMS), whole(1, ATOMS), whole(LATER_ROWS, 128)],
        out_specs=slots(COMPS * RH, ATOMS),
        out_shape=jax.ShapeDtypeStruct((K, COMPS * RH, ATOMS), bf16),
        scratch_shapes=[pltpu.VMEM((K, GEO_ROWS, ATOMS), f32)],
        compiler_params=params(("arbitrary",)),
        cost_estimate=pl.CostEstimate(
            flops=2 * 4096 * 256 * WIDTH, bytes_accessed=9_000_000, transcendentals=600_000
        ),
        name="probe_weights",
    )(vectors, count, pack)


HOLDERS = (2, 3, 4, 5, 7, 6)


def column_root(slab_ref):
    return slab_ref[lax.axis_index("gx") * lax.axis_size("gy") + lax.axis_index("gy")]


def collect_kernel(slab_ref, *refs):
    *block_refs, low_ref, high_ref, rest_ref, out_ref = refs
    code = lax.axis_index("gz") ^ column_root(slab_ref)

    @pl.when(code == 0)
    def _():
        out_ref[...] = low_ref[...]

    @pl.when(code == 1)
    def _():
        out_ref[...] = high_ref[...]

    for block, holder in enumerate(HOLDERS):

        @pl.when(code == holder)
        def _(block=block, holder=holder):
            out_ref[:FACE, :] = block_refs[SENT.index(block)][:FACE, :]
            if holder == 6:
                out_ref[FACE:, :] = block_refs[SENT.index(4)][FACE:, :]
            elif holder == 2:
                out_ref[FACE:, :] = rest_ref[...]
            else:
                out_ref[FACE:, :] = jnp.zeros((REST, COMPS * RH), bf16)


def collect(slab, blocks, low, high, rest):
    return pl.pallas_call(
        collect_kernel,
        in_specs=[pl.BlockSpec(memory_space=pltpu.SMEM)] + in_vmem(BLOCKS + 3),
        out_specs=pl.BlockSpec(memory_space=pltpu.VMEM),
        out_shape=jax.ShapeDtypeStruct((PART, COMPS * RH), bf16),
        compiler_params=params(),
        name="collect",
    )(slab, *[blocks[b] for b in SENT], low, high, rest)


def readout_kernel(slab_ref, idx_ref, weight_ref, near_ref, far_ref, out_ref, keys_ref):
    root = column_root(slab_ref)
    code = lax.axis_index("gz") ^ root

    def fetch(at, rows, holder, start):
        place = code ^ holder
        start = pl.multiple_of(place // 2 * PART + start, REST)

        @pl.when(place % 2 == 0)
        def _():
            keys_ref[pl.ds(at, rows), :] = near_ref[pl.ds(start, rows), :]

        @pl.when(place % 2 == 1)
        def _():
            keys_ref[pl.ds(at, rows), :] = far_ref[pl.ds(start, rows), :]

    fetch(0, PART, 0, 0)
    fetch(PART, PART, 1, 0)
    fetch(2 * PART, REST, 6, FACE)
    fetch(2 * PART + REST, REST, 2, FACE)
    for block, holder in enumerate(HOLDERS):
        odd = (parity(0), parity(1), root % 2)[block // 2]
        face = jnp.where(odd == block % 2, block // 2 * 2 + 1, block // 2 * 2)
        at = pl.multiple_of(ATOMS + face * FACE, FACE)
        fetch(at, FACE, holder, 0)
    rows = lax.broadcasted_iota(jnp.int32, (TABLE, ATOMS), 0)

    def one_step(step, total):
        first = step * WIDE
        weight = jnp.concatenate([weight_ref[first + s] for s in range(WIDE)], axis=1)
        product = dot(keys_ref[...], weight)
        for s in range(WIDE):
            chosen = rows == idx_ref[pl.ds(first + s, 1), :]
            part = jnp.where(chosen, product[:, s * ATOMS : (s + 1) * ATOMS], 0.0)
            total = total + jnp.sum(part.reshape(TABLE // 8, 8, ATOMS), axis=0)
        return total

    total = lax.fori_loop(0, STEPS, one_step, jnp.zeros((8, ATOMS), f32))
    out_ref[...] = jnp.sum(total, axis=0, keepdims=True)


def readout(slab, idx, weight, near, far):
    return pl.pallas_call(
        readout_kernel,
        in_specs=[pl.BlockSpec(memory_space=pltpu.SMEM)] + in_vmem(4),
        out_specs=pl.BlockSpec(memory_space=pltpu.VMEM),
        scratch_shapes=[pltpu.VMEM((TABLE, COMPS * RH), bf16)],
        out_shape=jax.ShapeDtypeStruct((1, ATOMS), f32),
        compiler_params=params(),
        name="readout",
    )(slab, idx, weight, near, far)


def exchange(blocks):
    landed = [None] * BLOCKS
    for block in SENT:
        axis, turn = AXES[block // 2], block % 2
        count = lax.axis_size(axis)
        pairs = [(i, partner(i, count, turn)) for i in range(count)]
        landed[block] = lax.ppermute(blocks[block], axis, pairs)
    return landed


def along_column(block, code):
    return lax.ppermute(block, "gz", [(i, i ^ code) for i in range(lax.axis_size("gz"))])


def column_keys(slab, blocks, low, high, rest, probe_weight):
    landed = [None] * BLOCKS
    inner = lax.axis_size("gz")
    for block in SENT:
        axis, turn, holder = AXES[block // 2], block % 2, HOLDERS[block]
        outer = lax.axis_size(axis)
        if axis == "gz":
            pairs = [(i, partner(i, inner, turn) ^ holder) for i in range(inner)]
            landed[block] = lax.ppermute(blocks[block], axis, pairs)
        else:
            pairs = [
                (i * inner + j, partner(i, outer, turn) * inner + (j ^ holder))
                for i in range(outer)
                for j in range(inner)
            ]
            landed[block] = lax.ppermute(blocks[block], (axis, "gz"), pairs)
    mine = collect(slab, landed, low, along_column(high, 1), along_column(rest, 2))
    moved = [along_column(mine, code) for code in (6, 4, 2)][::-1]
    *moved, probe_weight = lax.optimization_barrier((*moved, probe_weight))
    near = jnp.concatenate([mine] + moved, axis=0)
    return near, along_column(near, 1), probe_weight


def local(
    features,
    species,
    octant_lists,
    neighbour_index,
    neighbour_count,
    edge_vectors,
    radial_in,
    species_emb,
    radial_mid,
    radial_out,
    mix_weight,
    gate_weight,
    probe_in,
    probe_mid,
    probe_proj,
    probe_vectors,
    probe_index,
    probe_count,
    slab_index,
):
    sel, *blocks = pick(octant_lists, features)
    ghosts = exchange(blocks)
    species_row = species.reshape(1, ATOMS)
    geo, first, later = prepare(
        (
            neighbour_index,
            edge_vectors,
            neighbour_count.reshape(1, ATOMS),
            features,
            species_row,
            sel,
            radial_in,
            jnp.swapaxes(species_emb, 1, 2),
            radial_mid,
            radial_out,
            mix_weight,
            gate_weight,
            jnp.swapaxes(probe_proj, 1, 2),
            probe_in,
            probe_mid,
        )
    )
    for t in range(LAYERS):
        if t == 0:
            outs = layer(t, geo, first, ghosts, ())
        else:
            outs = layer(t, geo, later, ghosts, (turned, hidden_units(t, species_row, geo, later)))
        if t < LAYERS - 1:
            turned = outs[0]
            ghosts = exchange(outs[1:])
    near, far, probe_weight = column_keys(
        slab_index,
        outs[1:7],
        outs[7],
        outs[8],
        outs[9],
        probe_weights(probe_vectors, probe_count.reshape(1, ATOMS), later),
    )
    density = readout(slab_index, probe_index, probe_weight, near, far)
    return (outs[0], density.reshape(ATOMS))


def solution(mesh):
    in_specs = (
        P(("gx", "gy", "gz"), None),
        P(("gx", "gy", "gz")),
        P(None, None, None, ("gx", "gy", "gz")),
        P(None, ("gx", "gy", "gz")),
        P(("gx", "gy", "gz")),
        P(None, None, ("gx", "gy", "gz")),
        P(),
        P(),
        P(),
        P(),
        P(),
        P(),
        P(),
        P(),
        P(),
        P(None, None, ("gx", "gy", "gz")),
        P(None, ("gx", "gy", "gz")),
        P(("gx", "gy", "gz")),
        P(),
    )
    out_specs = (P(("gx", "gy", "gz"), None), P(("gx", "gy", "gz")))
    return jax.shard_map(local, mesh=mesh, in_specs=in_specs, out_specs=out_specs, check_vma=False)
```
